512 devices in a mesh: freq: 16 (over y, x), patch: 32 (over z, core).
Axes of the slice: x: 4, y: 4, z: 16, core: 2. Of those that a mesh axis runs over, the one named last changes fastest.
Arguments:
- responses: bfloat16 [2048, 2, 2048], P('patch', None, 'freq'), may hold values from -6 to 6
- adjoints: bfloat16 [2048, 2, 2048], P('patch', None, 'freq'), may hold values from -6 to 6
- patch_shapes: bfloat16 [3072, 4, 48, 128], P('patch'), may hold values from -0.25 to 0.25
- block_lists: int32 [3072, 4], P('patch'), may hold values from 0 to 15
- block_counts: int32 [3072], P('patch'), may hold values from 1 to 4
- patch_sizes: int32 [3072], P('patch'), may hold values from 12 to 48
- owner_map: int32 [3072], P('patch'), may hold values from 0 to 3071, each once
Outputs:
- loss_gradient: float32 [3072], P('patch')
The draws below stay inside these ranges and needn't reach their ends.
Inputs may be any that keep to these rules, and one draw needn't show every extreme that they name: `owner_map`: each patch appears once.
All inputs are finite; a program needn't handle non-finite values.
Results may differ from the reference program's by a relative error of at most 0.0003.
Values may be sent and summed in bfloat16 or wider, within the bound.
A program may use at most 64 MiB of HBM per device.

```python
import jax
import jax.numpy as jnp
from jax import lax

FREQS = 2048
MODES = 2048
BLOCK = 128
MBLOCKS = 16
SAMPLES = 48
SLOTS = 4
PATCHES = 3072


def with_ends(entries, rng, low, high):
    index_at = [jax.random.randint(jax.random.fold_in(rng, axis), (), 0, length) for axis, length in enumerate(entries.shape)]
    main_axis = entries.shape.index(max(entries.shape))
    next_to = index_at[:main_axis] + [(index_at[main_axis] + 1) % entries.shape[main_axis]] + index_at[main_axis + 1:]
    return entries.at[tuple(index_at)].set(low).at[tuple(next_to)].set(high)


def levels(own_key, extent, shards, low, largest):
    def one(axis_at, shards_of):
        draws = jax.random.uniform(jax.random.fold_in(jax.random.fold_in(own_key, 6), axis_at), (shards_of,), jnp.float32, low / len(shards), largest / len(shards))
        return jnp.repeat(jnp.exp(draws), extent[axis_at] // shards_of).reshape((-1,) + (1,) * (len(extent) - axis_at - 1))

    level = one(*shards[0])
    for cut in shards[1:]:
        level = level * one(*cut)
    return level


def noise(rng, dims, width, most, shards=(), kind=jnp.bfloat16):
    gain = levels(rng, dims, shards, -0.22, 0.18) if shards else 1.0
    result = jax.random.normal(rng, dims, jnp.float32) * width * gain
    return jnp.minimum(jnp.maximum(result, -most), most).astype(kind)


def setup_inputs(seed: int = 0) -> dict:
    key_of = jax.random.split(jax.random.key(seed), 8)
    responses = noise(key_of[0], (FREQS, 2, MODES), 1.0, 6.0, ((0, 32), (2, 16)))
    adjoints = noise(key_of[1], (FREQS, 2, MODES), 1.0, 6.0, ((0, 32), (2, 16)))
    patch_shapes = noise(key_of[2], (PATCHES, SLOTS, SAMPLES, BLOCK), (SLOTS * BLOCK) ** -0.5, 0.25, ((0, 32),))
    block_lists = with_ends(jax.random.randint(key_of[3], (PATCHES, SLOTS), 0, MBLOCKS), jax.random.fold_in(key_of[3], 1), 0, MBLOCKS - 1).astype(jnp.int32)
    block_counts = with_ends(jax.random.randint(key_of[4], (PATCHES,), 1, SLOTS + 1), jax.random.fold_in(key_of[4], 1), 1, SLOTS).astype(jnp.int32)
    patch_sizes = with_ends(jax.random.randint(key_of[5], (PATCHES,), SAMPLES // 4, SAMPLES + 1), jax.random.fold_in(key_of[5], 1), SAMPLES // 4, SAMPLES).astype(jnp.int32)
    owner_map = jax.random.permutation(key_of[6], PATCHES).astype(jnp.int32)
    return {"responses": responses, "adjoints": adjoints, "patch_shapes": patch_shapes, "block_lists": block_lists, "block_counts": block_counts, "patch_sizes": patch_sizes, "owner_map": owner_map}


def reference(responses, adjoints, patch_shapes, block_lists, block_counts, patch_sizes, owner_map):
    slot_live = jnp.arange(SLOTS, dtype=jnp.int32)[None, :] < block_counts[:, None]
    row_live = jnp.arange(SAMPLES, dtype=jnp.int32)[None, :] < patch_sizes[:, None]
    live = (slot_live[:, :, None, None] & row_live[:, None, :, None]).astype(jnp.bfloat16)
    masked = patch_shapes * live
    resp = responses.astype(jnp.float32).reshape(FREQS * 2, MBLOCKS, BLOCK)
    adjo = adjoints.astype(jnp.float32).reshape(FREQS * 2, MBLOCKS, BLOCK)
    group = 16

    def one(index):
        start = (index * group).astype(jnp.int32)
        blocks = lax.dynamic_slice_in_dim(block_lists, start, group, 0)
        shapes = lax.dynamic_slice_in_dim(masked, start, group, 0).astype(jnp.float32)
        forward = jnp.einsum("pksb,cpkb->cps", shapes, resp[:, blocks, :], precision=lax.Precision.HIGHEST)
        backward = jnp.einsum("pksb,cpkb->cps", shapes, adjo[:, blocks, :], precision=lax.Precision.HIGHEST)
        forward = forward.reshape(FREQS, 2, group, SAMPLES)
        backward = backward.reshape(FREQS, 2, group, SAMPLES)
        cross = forward[:, 0] * backward[:, 1] - forward[:, 1] * backward[:, 0]
        return jnp.sum(cross, axis=(0, 2))

    terms = lax.map(one, jnp.arange(PATCHES // group, dtype=jnp.int32)).reshape(PATCHES)
    scale = (SAMPLES * FREQS) ** -0.5
    return jnp.zeros((PATCHES,), jnp.float32).at[owner_map].set(terms * scale)
```

```python
import functools

import jax
import jax.numpy as jnp
from jax import lax
from jax.experimental import pallas as pl
from jax.experimental.pallas import tpu as pltpu
from jax.sharding import PartitionSpec as P

MESH = pl.DeviceIdType.MESH
F32 = jnp.float32
BF16 = jnp.bfloat16

PLANE = 16
COLUMN = 32
RING = 16
HOPS = 8
PATCHES = 96
SLOTS = 4
SAMPLES = 48
WIDTH = 128
PIECE = 16
QUARTERS = 4
UNROLL = 8


def from_left(hop):
    return 2 * hop - 1


def from_right(hop):
    return 2 * hop


def kernel(
    scale,
    resp_ref,
    adjo_ref,
    lists_ref,
    counts_ref,
    sizes_ref,
    owner_ref,
    shapes_hbm,
    out_ref,
    staged,
    x0,
    x1,
    x2,
    x3,
    shapes,
    acc,
    folded,
    dense,
    got_column,
    row,
    got_plane,
    shapes_sem,
    mix_send,
    mix_recv,
    right_send,
    left_send,
    right_recv,
    left_recv,
    pair_send,
    pair_recv,
    column_send,
    column_recv,
    plane_send,
    plane_recv,
):
    quarters = (x0, x1, x2, x3)
    q = lax.axis_index("freq")
    p = lax.axis_index("patch")
    right = (q, lax.rem(p + 2, COLUMN))
    left = (q, lax.rem(p + COLUMN - 2, COLUMN))
    pair = (q, p + 1 - 2 * lax.rem(p, 2))

    fetch = pltpu.make_async_copy(shapes_hbm, shapes, shapes_sem)
    fetch.start()

    barrier = pltpu.get_barrier_semaphore()

    def greet_column(d, carry):
        pl.semaphore_signal(barrier, inc=1, device_id=(q, lax.rem(p + d, COLUMN)), device_id_type=MESH)
        return carry

    def greet_plane(d, carry):
        pl.semaphore_signal(barrier, inc=1, device_id=(lax.rem(q + d, PLANE), p), device_id_type=MESH)
        return carry

    lax.fori_loop(1, PLANE, greet_plane, 0)
    lax.fori_loop(1, COLUMN, greet_column, 0)

    resp = resp_ref[...].astype(F32).reshape(PLANE, 8, WIDTH)
    adjo = adjo_ref[...].astype(F32)
    odd = lax.broadcasted_iota(jnp.int32, adjo.shape, 0) % 2 == 1
    rows = adjo.shape[0]
    swapped = jnp.where(odd, -pltpu.roll(adjo, 1, 0), pltpu.roll(adjo, rows - 1, 0)).reshape(PLANE, 8, WIDTH)
    staged[...] = jnp.concatenate([resp, swapped], axis=1).astype(BF16)
    for x in quarters:
        x[PLANE] = jnp.zeros(x.shape[1:], BF16)
    x0[q, 0, 0] = staged[q]

    pl.semaphore_wait(barrier, PLANE - 1 + COLUMN - 1)

    def mix(d):
        there = lax.rem(q + d, PLANE)
        return pltpu.make_async_remote_copy(
            src_ref=staged.at[there],
            dst_ref=x0.at[q, 0, 0],
            send_sem=mix_send.at[d - 1],
            recv_sem=mix_recv,
            device_id=(there, p),
            device_id_type=MESH,
        )

    def mix_start(d, carry):
        mix(d).start()
        return carry

    lax.fori_loop(1, PLANE, mix_start, 0)

    owner_row = owner_ref[...].astype(F32)
    eye = lax.broadcasted_iota(jnp.int32, (PATCHES, PATCHES), 0) == lax.broadcasted_iota(jnp.int32, (PATCHES, PATCHES), 1)
    owner_column = jnp.sum(jnp.where(eye, jnp.broadcast_to(owner_row, (PATCHES, PATCHES)), 0.0), axis=1, keepdims=True)
    first = lax.broadcasted_iota(jnp.int32, (COLUMN, PATCHES), 0).astype(F32) * PATCHES
    owner_rows = jnp.broadcast_to(owner_row, (COLUMN, PATCHES))
    to_device = jnp.where((owner_rows >= first) & (owner_rows < first + PATCHES), 1.0, 0.0).astype(BF16)
    place = owner_column - jnp.floor((owner_column + 0.5) * (1.0 / PATCHES)) * PATCHES
    lane = lax.broadcasted_iota(jnp.int32, (PATCHES, WIDTH), 1).astype(F32)
    to_lane = jnp.where(place == lane, 1.0, 0.0)

    def chunk(core, slot, part=None):
        x = quarters[slot // QUARTERS]
        blocks = pl.ds(0, PLANE) if part is None else pl.ds(part * (PLANE // 2), PLANE // 2)
        return x.at[blocks, core, slot % QUARTERS]

    def to_right(hop, part):
        source = 0 if hop == 1 else from_left(hop - 1)
        target = from_left(hop) if hop < HOPS else 2 * HOPS - 1
        return pltpu.make_async_remote_copy(
            src_ref=chunk(0, source, part),
            dst_ref=chunk(0, target, part),
            send_sem=right_send.at[hop - 1, part],
            recv_sem=right_recv.at[hop - 1, part],
            device_id=right,
            device_id_type=MESH,
        )

    def to_left(hop, part):
        source = 0 if hop == 1 else from_right(hop - 1)
        target = from_right(hop) if hop < HOPS else 2 * HOPS - 1
        return pltpu.make_async_remote_copy(
            src_ref=chunk(0, source, part),
            dst_ref=chunk(0, target, part),
            send_sem=left_send.at[hop - 1, part],
            recv_sem=left_recv.at[hop - 1, part],
            device_id=left,
            device_id_type=MESH,
        )

    def to_pair(slot):
        return pltpu.make_async_remote_copy(
            src_ref=chunk(0, slot),
            dst_ref=chunk(1, slot),
            send_sem=pair_send.at[slot],
            recv_sem=pair_recv.at[slot],
            device_id=pair,
            device_id_type=MESH,
        )

    def goes_right(hop, part):
        return hop < HOPS or (hop == HOPS and part == 0)

    def goes_left(hop, part):
        return hop < HOPS or (hop == HOPS and part == 1)

    sample = lax.broadcasted_iota(jnp.int32, (SAMPLES, WIDTH), 0)

    def patch(quarter, index):
        x = quarters[quarter]
        live = counts_ref[index]
        sides = []
        for k in range(SLOTS):
            block = jnp.where(k < live, lists_ref[index * SLOTS + k], PLANE)
            sides.append(x[block].reshape(WIDTH, WIDTH))
        columns = jnp.concatenate(sides, axis=1)
        strain = jnp.concatenate([shapes[index, k] for k in range(SLOTS)], axis=1)
        both = lax.dot_general(strain, columns, (((1,), (1,)), ((), ())), preferred_element_type=F32)
        cross = both * pltpu.roll(both, WIDTH - 8, 1)
        cross = jnp.where(sample < sizes_ref[index], cross, 0.0)
        part = jnp.sum(cross.reshape(SAMPLES // 8, 8, WIDTH), axis=0)
        if quarter == 0:
            acc[index] = part
        elif quarter < QUARTERS - 1:
            acc[index] += part
        else:
            folded[index] = jnp.sum(acc[index] + part, axis=0, keepdims=True)

    def work(quarter, share, shares):
        turns = PATCHES // UNROLL // shares

        def turn(step, carry):
            for u in range(UNROLL):
                patch(quarter, step * UNROLL + u)
            return carry

        lax.fori_loop(share * turns, (share + 1) * turns, turn, 0)

    def mix_wait():
        pltpu.make_async_copy(x0.at[pl.ds(0, PLANE - 1), 0, 0], x0.at[pl.ds(0, PLANE - 1), 0, 0], mix_recv).wait()

    mix_wait()
    for part in range(2):
        to_right(1, part).start()
        to_left(1, part).start()
    to_pair(0).start()
    fetch.wait()

    queue = []
    for hop in range(1, HOPS + 1):
        for part in range(2):
            if goes_right(hop, part):
                to_right(hop, part).wait_recv()
                if goes_right(hop + 1, part):
                    to_right(hop + 1, part).start()
            if goes_left(hop, part):
                to_left(hop, part).wait_recv()
                if goes_left(hop + 1, part):
                    to_left(hop + 1, part).start()
            if part == 1:
                slots = (from_left(hop), from_right(hop)) if hop < HOPS else (2 * HOPS - 1,)
                for slot in slots:
                    to_pair(slot).start()
                    if slot % QUARTERS == QUARTERS - 1:
                        queue.extend((slot // QUARTERS, share) for share in range(4))
            if queue:
                quarter, share = queue.pop(0)
                if share == 0:
                    for slot in range(quarter * QUARTERS, (quarter + 1) * QUARTERS):
                        to_pair(slot).wait_recv()
                work(quarter, share, 4)
    while queue:
        quarter, share = queue.pop(0)
        if share == 0:
            for slot in range(quarter * QUARTERS, (quarter + 1) * QUARTERS):
                to_pair(slot).wait_recv()
            shares = 1
            queue = [entry for entry in queue if entry[0] != quarter]
            work(quarter, 0, 1)
        else:
            work(quarter, share, 4)

    lanes = lax.broadcasted_iota(jnp.int32, (PATCHES, WIDTH), 1)
    terms = jnp.where(lanes // 8 % 2 == 0, folded[...].reshape(PATCHES, WIDTH), 0.0)
    terms = jnp.sum(terms, axis=1, keepdims=True) * scale
    spread = terms * to_lane
    high = spread.astype(BF16)
    rest = spread - high.astype(F32)
    middle = rest.astype(BF16)
    low = (rest - middle.astype(F32)).astype(BF16)
    placed = sum(
        lax.dot_general(to_device, piece, (((1,), (0,)), ((), ())), preferred_element_type=F32)
        for piece in (low, middle, high)
    )
    dense[...] = placed.reshape(COLUMN, 1, WIDTH)

    def column(d):
        there = lax.rem(p + d, COLUMN)
        return pltpu.make_async_remote_copy(
            src_ref=dense.at[there],
            dst_ref=got_column.at[d - 1],
            send_sem=column_send.at[d - 1],
            recv_sem=column_recv,
            device_id=(q, there),
            device_id_type=MESH,
        )

    def column_start(d, carry):
        column(d).start()
        return carry

    lax.fori_loop(1, COLUMN, column_start, 0)
    pltpu.make_async_copy(got_column, got_column, column_recv).wait()
    row[...] = dense[p] + jnp.sum(got_column[...], axis=0)

    def plane(d):
        return pltpu.make_async_remote_copy(
            src_ref=row,
            dst_ref=got_plane.at[d - 1],
            send_sem=plane_send.at[d - 1],
            recv_sem=plane_recv,
            device_id=(lax.rem(q + d, PLANE), p),
            device_id_type=MESH,
        )

    def plane_start(d, carry):
        plane(d).start()
        return carry

    lax.fori_loop(1, PLANE, plane_start, 0)
    pltpu.make_async_copy(got_plane, got_plane, plane_recv).wait()
    total = row[...] + jnp.sum(got_plane[...], axis=0)
    out_ref[...] = total[:, :PATCHES]

    def mix_sent(d, carry):
        mix(d).wait_send()
        return carry

    def column_sent(d, carry):
        column(d).wait_send()
        return carry

    def plane_sent(d, carry):
        plane(d).wait_send()
        return carry

    lax.fori_loop(1, PLANE, mix_sent, 0)
    for hop in range(1, HOPS + 1):
        for part in range(2):
            if goes_right(hop, part):
                to_right(hop, part).wait_send()
            if goes_left(hop, part):
                to_left(hop, part).wait_send()
    for slot in range(2 * HOPS):
        to_pair(slot).wait_send()
    lax.fori_loop(1, COLUMN, column_sent, 0)
    lax.fori_loop(1, PLANE, plane_sent, 0)


def body(responses, adjoints, patch_shapes, block_lists, block_counts, patch_sizes, owner_map):
    freqs = responses.shape[0] * COLUMN
    scale = (SAMPLES * freqs) ** (-0.5)
    vmem = pl.BlockSpec(memory_space=pltpu.VMEM)
    smem = pl.BlockSpec(memory_space=pltpu.SMEM)
    quarter = pltpu.VMEM((PLANE + 1, 2, QUARTERS, PIECE, WIDTH), BF16)
    dma = pltpu.SemaphoreType.DMA
    rows = responses.shape[0] * 2
    out = pl.pallas_call(
        functools.partial(kernel, scale),
        out_shape=jax.ShapeDtypeStruct((1, PATCHES), F32),
        in_specs=[vmem, vmem, smem, smem, smem, vmem, pl.BlockSpec(memory_space=pl.ANY)],
        out_specs=vmem,
        scratch_shapes=[
            pltpu.VMEM((PLANE, PIECE, WIDTH), BF16),
            quarter,
            quarter,
            quarter,
            quarter,
            pltpu.VMEM(patch_shapes.shape, BF16),
            pltpu.VMEM((PATCHES, 8, WIDTH), F32),
            pltpu.VMEM((PATCHES, 1, WIDTH), F32),
            pltpu.VMEM((COLUMN, 1, WIDTH), F32),
            pltpu.VMEM((COLUMN - 1, 1, WIDTH), F32),
            pltpu.VMEM((1, WIDTH), F32),
            pltpu.VMEM((PLANE - 1, 1, WIDTH), F32),
            dma,
            dma((PLANE - 1,)),
            dma,
            dma((HOPS, 2)),
            dma((HOPS, 2)),
            dma((HOPS, 2)),
            dma((HOPS, 2)),
            dma((2 * HOPS,)),
            dma((2 * HOPS,)),
            dma((COLUMN - 1,)),
            dma,
            dma((PLANE - 1,)),
            dma,
        ],
        compiler_params=pltpu.CompilerParams(
            collective_id=0, has_side_effects=True, vmem_limit_bytes=32 * 1024 * 1024
        ),
        cost_estimate=pl.CostEstimate(flops=2415919104, bytes_accessed=5000000, transcendentals=0),
    )(
        responses.reshape(rows, WIDTH),
        adjoints.reshape(rows, WIDTH),
        block_lists.reshape(-1),
        block_counts,
        patch_sizes,
        owner_map.reshape(1, -1),
        patch_shapes,
    )
    return out.reshape(-1)


def solution(mesh):
    placed = (
        P("patch", None, "freq"),
        P("patch", None, "freq"),
        P("patch", None, None, None),
        P("patch", None),
        P("patch"),
        P("patch"),
        P("patch"),
    )
    return jax.shard_map(body, mesh=mesh, in_specs=placed, out_specs=P("patch"), check_vma=False)
```

```python
import functools

import jax
import jax.numpy as jnp
from jax import lax
from jax.experimental import pallas as pl
from jax.experimental.pallas import tpu as pltpu
from jax.sharding import PartitionSpec as P

MESH = pl.DeviceIdType.MESH
F32 = jnp.float32
BF16 = jnp.bfloat16

PLANE = 16
COLUMN = 32
RING = 16
PATCHES = 96
SLOTS = 4
SAMPLES = 48
WIDTH = 128
PIECE = 16
QUARTERS = 4
UNROLL = 16


EDGES = ((0, 1), (0, 3), (1, 2), (3, 4), (3, 6), (4, 5), (6, 7), (7, 8))
FAR = RING // 2
ARRIVAL = (1, 3, 2, 4, 6, 5, 7)


def slot_of(distance, side):
    if distance == 0:
        return 0
    if distance == FAR:
        return 2 * FAR - 1
    return 1 + 2 * ARRIVAL.index(distance) + side


def kernel(
    scale,
    resp_ref,
    adjo_ref,
    lists_ref,
    counts_ref,
    sizes_ref,
    owner_ref,
    shapes_hbm,
    out_ref,
    staged,
    x0,
    x1,
    x2,
    x3,
    turned0,
    turned1,
    shapes,
    acc,
    folded,
    dense,
    got_column,
    row,
    got_plane,
    shapes_sem,
    mix_send,
    mix_recv,
    ring_send,
    ring_recv,
    far_send,
    far_recv,
    pair_send,
    pair_recv,
    column_send,
    column_recv,
    plane_send,
    plane_recv,
):
    quarters = (x0, x1, x2, x3)
    halves = (turned0, turned1)
    q = lax.axis_index("freq")
    p = lax.axis_index("patch")
    pair = (q, p + 1 - 2 * lax.rem(p, 2))

    fetch = pltpu.make_async_copy(shapes_hbm, shapes, shapes_sem)
    fetch.start()

    barrier = pltpu.get_barrier_semaphore()

    def greet_column(d, carry):
        pl.semaphore_signal(barrier, inc=1, device_id=(q, lax.rem(p + d, COLUMN)), device_id_type=MESH)
        return carry

    def greet_plane(d, carry):
        pl.semaphore_signal(barrier, inc=1, device_id=(lax.rem(q + d, PLANE), p), device_id_type=MESH)
        return carry

    lax.fori_loop(1, PLANE, greet_plane, 0)
    lax.fori_loop(1, COLUMN, greet_column, 0)

    resp = resp_ref[...].astype(F32).reshape(PLANE, 8, WIDTH)
    adjo = adjo_ref[...].astype(F32)
    odd = lax.broadcasted_iota(jnp.int32, adjo.shape, 0) % 2 == 1
    rows = adjo.shape[0]
    swapped = jnp.where(odd, -pltpu.roll(adjo, 1, 0), pltpu.roll(adjo, rows - 1, 0)).reshape(PLANE, 8, WIDTH)
    staged[...] = jnp.concatenate([resp, swapped], axis=1).astype(BF16)
    for turned in halves:
        turned[PLANE] = jnp.zeros(turned.shape[1:], BF16)
    x0[q, 0, 0] = staged[q]

    pl.semaphore_wait(barrier, PLANE - 1 + COLUMN - 1)

    def mix(d):
        there = lax.rem(q + d, PLANE)
        return pltpu.make_async_remote_copy(
            src_ref=staged.at[there],
            dst_ref=x0.at[q, 0, 0],
            send_sem=mix_send.at[d - 1],
            recv_sem=mix_recv,
            device_id=(there, p),
            device_id_type=MESH,
        )

    def mix_start(d, carry):
        mix(d).start()
        return carry

    lax.fori_loop(1, PLANE, mix_start, 0)

    owner_row = owner_ref[...].astype(F32)
    eye = lax.broadcasted_iota(jnp.int32, (PATCHES, PATCHES), 0) == lax.broadcasted_iota(jnp.int32, (PATCHES, PATCHES), 1)
    owner_column = jnp.sum(jnp.where(eye, jnp.broadcast_to(owner_row, (PATCHES, PATCHES)), 0.0), axis=1, keepdims=True)
    first = lax.broadcasted_iota(jnp.int32, (COLUMN, PATCHES), 0).astype(F32) * PATCHES
    owner_rows = jnp.broadcast_to(owner_row, (COLUMN, PATCHES))
    to_device = jnp.where((owner_rows >= first) & (owner_rows < first + PATCHES), 1.0, 0.0).astype(BF16)
    place = owner_column - jnp.floor((owner_column + 0.5) * (1.0 / PATCHES)) * PATCHES
    lane = lax.broadcasted_iota(jnp.int32, (PATCHES, WIDTH), 1).astype(F32)
    to_lane = jnp.where(place == lane, 1.0, 0.0)

    def chunk(core, slot, part=None):
        x = quarters[slot // QUARTERS]
        blocks = pl.ds(0, PLANE) if part is None else pl.ds(part * (PLANE // 2), PLANE // 2)
        return x.at[blocks, core, slot % QUARTERS]

    def along(side, edge, part):
        near, far = EDGES[edge]
        step = 2 * (far - near) * (1 - 2 * side)
        return pltpu.make_async_remote_copy(
            src_ref=chunk(0, slot_of(near, side), part),
            dst_ref=chunk(0, slot_of(far, side), part),
            send_sem=ring_send.at[side, edge, part],
            recv_sem=ring_recv.at[side, edge, part],
            device_id=(q, lax.rem(p + COLUMN + step, COLUMN)),
            device_id_type=MESH,
        )

    def to_far_pair(side):
        last = slot_of(FAR, side)
        return pltpu.make_async_remote_copy(
            src_ref=chunk(0, slot_of(FAR - 1, side), side),
            dst_ref=chunk(1, last, side),
            send_sem=far_send.at[side],
            recv_sem=far_recv.at[side],
            device_id=(q, lax.rem(pair[1] + COLUMN + 2 * (1 - 2 * side), COLUMN)),
            device_id_type=MESH,
        )

    def to_pair(slot):
        return pltpu.make_async_remote_copy(
            src_ref=chunk(0, slot),
            dst_ref=chunk(1, slot),
            send_sem=pair_send.at[slot],
            recv_sem=pair_recv.at[slot],
            device_id=pair,
            device_id_type=MESH,
        )

    def taken(side, edge, part):
        return EDGES[edge][1] < FAR or part == side

    def send_on(side, distance, part):
        for edge, (near, far) in enumerate(EDGES):
            if near == distance and taken(side, edge, part):
                along(side, edge, part).start()
                if far == FAR:
                    to_far_pair(side).start()

    sample = lax.broadcasted_iota(jnp.int32, (SAMPLES, WIDTH), 0)

    def patch(half, index):
        live = counts_ref[index]
        sides = []
        for k in range(SLOTS):
            block = jnp.where(k < live, lists_ref[k, index], PLANE)
            sides.append(halves[half][block])
        columns = jnp.concatenate(sides, axis=0)
        strain = jnp.concatenate([shapes[index, k] for k in range(SLOTS)], axis=1)
        both = jnp.dot(strain, columns, preferred_element_type=F32)
        cross = 0.0
        for at in (0, WIDTH):
            part = both[:, at : at + WIDTH]
            cross = cross + part * pltpu.roll(part, WIDTH - 8, 1)
        cross = jnp.where(sample < sizes_ref[index], cross, 0.0)
        part = jnp.sum(cross.reshape(SAMPLES // 8, 8, WIDTH), axis=0)
        if half == 0:
            acc[index] = part
        else:
            folded[index] = jnp.sum(acc[index] + part, axis=0, keepdims=True)

    def work(half, share, shares):
        turns = PATCHES // UNROLL // shares

        def turn(step, carry):
            for u in range(UNROLL):
                patch(half, step * UNROLL + u)
            return carry

        lax.fori_loop(share * turns, (share + 1) * turns, turn, 0)

    def pair_wait(slot):
        if slot == 2 * FAR - 1:
            for side in range(2):
                to_far_pair(side).wait_recv()
        else:
            to_pair(slot).wait_recv()

    def turn_over(quarter):
        for slot in range(quarter * QUARTERS, (quarter + 1) * QUARTERS):
            pair_wait(slot)
        x = quarters[quarter]
        turned = halves[quarter // 2]
        at = quarter % 2 * WIDTH

        def block(b, carry):
            turned[b, :, at : at + WIDTH] = x[b].reshape(WIDTH, WIDTH).T
            return carry

        lax.fori_loop(0, PLANE, block, 0)

    pltpu.make_async_copy(x0.at[pl.ds(0, PLANE - 1), 0, 0], x0.at[pl.ds(0, PLANE - 1), 0, 0], mix_recv).wait()
    for part in range(2):
        for side in range(2):
            send_on(side, 0, part)
    to_pair(0).start()

    tasks = {
        2: [lambda: turn_over(0), fetch.wait],
        4: [lambda: turn_over(1), lambda: work(0, 0, 6)],
        5: [lambda: work(0, 1, 6), lambda: work(0, 2, 6)],
        6: [lambda: work(0, 3, 6), lambda: turn_over(2), lambda: work(0, 4, 6), lambda: work(0, 5, 6)],
    }
    for edge, (_, far) in enumerate(EDGES):
        pending = list(tasks.get(edge, ()))
        for part in range(2):
            for side in range(2):
                if taken(side, edge, part):
                    along(side, edge, part).wait_recv()
                    if far < FAR:
                        send_on(side, far, part)
                        if part == 1:
                            to_pair(slot_of(far, side)).start()
            if part == 0 and len(pending) > 1 and edge > 3:
                pending.pop(0)()
        for task in pending:
            task()
    turn_over(3)
    work(1, 0, 1)

    lanes = lax.broadcasted_iota(jnp.int32, (PATCHES, WIDTH), 1)
    terms = jnp.where(lanes // 8 % 2 == 0, folded[...].reshape(PATCHES, WIDTH), 0.0)
    terms = jnp.sum(terms, axis=1, keepdims=True) * scale
    spread = terms * to_lane
    high = spread.astype(BF16)
    rest = spread - high.astype(F32)
    middle = rest.astype(BF16)
    low = (rest - middle.astype(F32)).astype(BF16)
    placed = sum(
        lax.dot_general(to_device, piece, (((1,), (0,)), ((), ())), preferred_element_type=F32)
        for piece in (low, middle, high)
    )
    dense[...] = placed.reshape(COLUMN, 1, WIDTH)

    def column(i):
        d = COLUMN // 2 + (1 - 2 * lax.rem(i, 2)) * lax.div(i, 2)
        there = lax.rem(p + d, COLUMN)
        return pltpu.make_async_remote_copy(
            src_ref=dense.at[there],
            dst_ref=got_column.at[d - 1],
            send_sem=column_send.at[d - 1],
            recv_sem=column_recv,
            device_id=(q, there),
            device_id_type=MESH,
        )

    def column_start(d, carry):
        column(d).start()
        return carry

    lax.fori_loop(1, COLUMN, column_start, 0)
    pltpu.make_async_copy(got_column, got_column, column_recv).wait()
    row[...] = dense[p] + jnp.sum(got_column[...], axis=0)

    def plane(d):
        return pltpu.make_async_remote_copy(
            src_ref=row,
            dst_ref=got_plane.at[d - 1],
            send_sem=plane_send.at[d - 1],
            recv_sem=plane_recv,
            device_id=(lax.rem(q + d, PLANE), p),
            device_id_type=MESH,
        )

    def plane_start(d, carry):
        plane(d).start()
        return carry

    lax.fori_loop(1, PLANE, plane_start, 0)
    pltpu.make_async_copy(got_plane, got_plane, plane_recv).wait()
    total = row[...] + jnp.sum(got_plane[...], axis=0)
    out_ref[...] = total[:, :PATCHES]

    def mix_sent(d, carry):
        mix(d).wait_send()
        return carry

    def column_sent(d, carry):
        column(d).wait_send()
        return carry

    def plane_sent(d, carry):
        plane(d).wait_send()
        return carry

    lax.fori_loop(1, PLANE, mix_sent, 0)
    for edge in range(len(EDGES)):
        for part in range(2):
            for side in range(2):
                if taken(side, edge, part):
                    along(side, edge, part).wait_send()
    for side in range(2):
        to_far_pair(side).wait_send()
    for slot in range(2 * FAR - 1):
        to_pair(slot).wait_send()
    lax.fori_loop(1, COLUMN, column_sent, 0)
    lax.fori_loop(1, PLANE, plane_sent, 0)


def body(responses, adjoints, patch_shapes, block_lists, block_counts, patch_sizes, owner_map):
    freqs = responses.shape[0] * COLUMN
    scale = (SAMPLES * freqs) ** (-0.5)
    vmem = pl.BlockSpec(memory_space=pltpu.VMEM)
    smem = pl.BlockSpec(memory_space=pltpu.SMEM)
    quarter = pltpu.VMEM((PLANE, 2, QUARTERS, PIECE, WIDTH), BF16)
    dma = pltpu.SemaphoreType.DMA
    rows = responses.shape[0] * 2
    out = pl.pallas_call(
        functools.partial(kernel, scale),
        out_shape=jax.ShapeDtypeStruct((1, PATCHES), F32),
        in_specs=[vmem, vmem, smem, smem, smem, vmem, pl.BlockSpec(memory_space=pl.ANY)],
        out_specs=vmem,
        scratch_shapes=[
            pltpu.VMEM((PLANE, PIECE, WIDTH), BF16),
            quarter,
            quarter,
            quarter,
            quarter,
            pltpu.VMEM((PLANE + 1, WIDTH, 2 * WIDTH), BF16),
            pltpu.VMEM((PLANE + 1, WIDTH, 2 * WIDTH), BF16),
            pltpu.VMEM(patch_shapes.shape, BF16),
            pltpu.VMEM((PATCHES, 8, WIDTH), F32),
            pltpu.VMEM((PATCHES, 1, WIDTH), F32),
            pltpu.VMEM((COLUMN, 1, WIDTH), F32),
            pltpu.VMEM((COLUMN - 1, 1, WIDTH), F32),
            pltpu.VMEM((1, WIDTH), F32),
            pltpu.VMEM((PLANE - 1, 1, WIDTH), F32),
            dma,
            dma((PLANE - 1,)),
            dma,
            dma((2, len(EDGES), 2)),
            dma((2, len(EDGES), 2)),
            dma((2,)),
            dma((2,)),
            dma((2 * FAR - 1,)),
            dma((2 * FAR - 1,)),
            dma((COLUMN - 1,)),
            dma,
            dma((PLANE - 1,)),
            dma,
        ],
        compiler_params=pltpu.CompilerParams(
            collective_id=0, has_side_effects=True, vmem_limit_bytes=58 * 1024 * 1024
        ),
        cost_estimate=pl.CostEstimate(flops=2415919104, bytes_accessed=5000000, transcendentals=0),
    )(
        responses.reshape(rows, WIDTH),
        adjoints.reshape(rows, WIDTH),
        block_lists.T,
        block_counts,
        patch_sizes,
        owner_map.reshape(1, -1),
        patch_shapes,
    )
    return out.reshape(-1)


def solution(mesh):
    placed = (
        P("patch", None, "freq"),
        P("patch", None, "freq"),
        P("patch", None, None, None),
        P("patch", None),
        P("patch"),
        P("patch"),
        P("patch"),
    )
    return jax.shard_map(body, mesh=mesh, in_specs=placed, out_specs=P("patch"), check_vma=False)
```

```python
import functools

import jax
import jax.numpy as jnp
from jax import lax
from jax.experimental import pallas as pl
from jax.experimental.pallas import tpu as pltpu
from jax.sharding import PartitionSpec as P

MESH = pl.DeviceIdType.MESH
F32 = jnp.float32
BF16 = jnp.bfloat16

PLANE = 16
COLUMN = 32
RING = 16
PATCHES = 96
SLOTS = 4
SAMPLES = 48
WIDTH = 128
PIECE = 16
QUARTERS = 4
UNROLL = 16


EDGES = ((2, 3), (2, 5), (3, 4), (5, 6), (6, 7), (7, 8))
REACH = 2
FAR = RING // 2
ARRIVAL = (1, 2, 3, 5, 4, 6, 7)


def slot_of(distance, side):
    if distance == 0:
        return 0
    if distance == FAR:
        return 2 * FAR - 1
    return 1 + 2 * ARRIVAL.index(distance) + side


def kernel(
    scale,
    resp_hbm,
    adjo_hbm,
    lists_hbm,
    counts_hbm,
    sizes_hbm,
    owner_hbm,
    shapes_hbm,
    out_ref,
    resp_ref,
    adjo_ref,
    lists_ref,
    counts_ref,
    sizes_ref,
    owner_ref,
    input_sem,
    staged,
    x0,
    x1,
    x2,
    x3,
    turned0,
    turned1,
    shapes,
    acc,
    folded,
    dense,
    got_column,
    row,
    got_plane,
    mix_send,
    mix_recv,
    ring_send,
    ring_recv,
    far_send,
    far_recv,
    pair_send,
    pair_recv,
    column_send,
    column_recv,
    plane_send,
    plane_recv,
):
    quarters = (x0, x1, x2, x3)
    halves = (turned0, turned1)
    q = lax.axis_index("freq")
    p = lax.axis_index("patch")
    pair = (q, p + 1 - 2 * lax.rem(p, 2))

    planes = tuple(sorted(range(-REACH, REACH + 1), key=lambda dz: -abs(dz)))

    def shifted(dz):
        return lax.rem(p + COLUMN + 2 * dz, COLUMN)

    inputs = [
        pltpu.make_async_copy(source, target, input_sem.at[at])
        for at, (source, target) in enumerate(
            (
                (resp_hbm, resp_ref),
                (adjo_hbm, adjo_ref),
                (owner_hbm, owner_ref),
                (lists_hbm, lists_ref),
                (counts_hbm, counts_ref),
                (sizes_hbm, sizes_ref),
                (shapes_hbm, shapes),
            )
        )
    ]
    for copy in inputs[:2]:
        copy.start()

    barrier = pltpu.get_barrier_semaphore()
    greeted = 0
    for dz in planes:

        def greet(d, carry, dz=dz):
            pl.semaphore_signal(barrier, inc=1, device_id=(lax.rem(q + d, PLANE), shifted(dz)), device_id_type=MESH)
            return carry

        lax.fori_loop(0 if dz else 1, PLANE, greet, 0)
        greeted += PLANE if dz else PLANE - 1
    for there in (pair, (q, shifted(3)), (q, shifted(-3)), (q, lax.rem(pair[1] + 2, COLUMN)), (q, lax.rem(pair[1] + COLUMN - 2, COLUMN))):
        pl.semaphore_signal(barrier, inc=1, device_id=there, device_id_type=MESH)
        greeted += 1
    for copy in inputs[2:]:
        copy.start()
    for copy in inputs[:2]:
        copy.wait()

    resp = resp_ref[...].astype(F32).reshape(PLANE, 8, WIDTH)
    adjo = adjo_ref[...].astype(F32)
    odd = lax.broadcasted_iota(jnp.int32, adjo.shape, 0) % 2 == 1
    rows = adjo.shape[0]
    swapped = jnp.where(odd, -pltpu.roll(adjo, 1, 0), pltpu.roll(adjo, rows - 1, 0)).reshape(PLANE, 8, WIDTH)
    staged[...] = jnp.concatenate([resp, swapped], axis=1).astype(BF16)
    x0[q, 0, 0] = staged[q]

    pl.semaphore_wait(barrier, greeted)

    def chunk(core, slot, part=None):
        x = quarters[slot // QUARTERS]
        blocks = pl.ds(0, PLANE) if part is None else pl.ds(part * (PLANE // 2), PLANE // 2)
        return x.at[blocks, core, slot % QUARTERS]

    def arrives(dz):
        return slot_of(abs(dz), 0 if dz > 0 else 1)

    for at, dz in enumerate(planes):

        def mix_start(d, carry, at=at, dz=dz):
            there = lax.rem(q + d, PLANE)
            slot = arrives(dz)
            pltpu.make_async_remote_copy(
                src_ref=staged.at[there],
                dst_ref=quarters[slot // QUARTERS].at[q, 0, slot % QUARTERS],
                send_sem=mix_send.at[at],
                recv_sem=mix_recv.at[at],
                device_id=(there, shifted(dz)),
                device_id_type=MESH,
            ).start()
            return carry

        lax.fori_loop(0 if dz else 1, PLANE, mix_start, 0)

    def mix_wait(at, dz, sems):
        pieces = staged if dz else staged.at[pl.ds(0, PLANE - 1)]
        pltpu.make_async_copy(pieces, pieces, sems.at[at]).wait()

    for turned in halves:
        turned[PLANE] = jnp.zeros(turned.shape[1:], BF16)
    inputs[2].wait()

    owner_row = owner_ref[...].astype(F32)
    eye = lax.broadcasted_iota(jnp.int32, (PATCHES, PATCHES), 0) == lax.broadcasted_iota(jnp.int32, (PATCHES, PATCHES), 1)
    owner_column = jnp.sum(jnp.where(eye, jnp.broadcast_to(owner_row, (PATCHES, PATCHES)), 0.0), axis=1, keepdims=True)
    first = lax.broadcasted_iota(jnp.int32, (COLUMN, PATCHES), 0).astype(F32) * PATCHES
    owner_rows = jnp.broadcast_to(owner_row, (COLUMN, PATCHES))
    to_device = jnp.where((owner_rows >= first) & (owner_rows < first + PATCHES), 1.0, 0.0).astype(BF16)
    place = owner_column - jnp.floor((owner_column + 0.5) * (1.0 / PATCHES)) * PATCHES
    lane = lax.broadcasted_iota(jnp.int32, (PATCHES, WIDTH), 1).astype(F32)
    to_lane = jnp.where(place == lane, 1.0, 0.0)

    def along(side, edge, part):
        near, far = EDGES[edge]
        step = 2 * (far - near) * (1 - 2 * side)
        return pltpu.make_async_remote_copy(
            src_ref=chunk(0, slot_of(near, side), part),
            dst_ref=chunk(0, slot_of(far, side), part),
            send_sem=ring_send.at[side, edge, part],
            recv_sem=ring_recv.at[side, edge, part],
            device_id=(q, lax.rem(p + COLUMN + step, COLUMN)),
            device_id_type=MESH,
        )

    def to_far_pair(side):
        last = slot_of(FAR, side)
        return pltpu.make_async_remote_copy(
            src_ref=chunk(0, slot_of(FAR - 1, side), side),
            dst_ref=chunk(1, last, side),
            send_sem=far_send.at[side],
            recv_sem=far_recv.at[side],
            device_id=(q, lax.rem(pair[1] + COLUMN + 2 * (1 - 2 * side), COLUMN)),
            device_id_type=MESH,
        )

    def to_pair(slot):
        return pltpu.make_async_remote_copy(
            src_ref=chunk(0, slot),
            dst_ref=chunk(1, slot),
            send_sem=pair_send.at[slot],
            recv_sem=pair_recv.at[slot],
            device_id=pair,
            device_id_type=MESH,
        )

    def taken(side, edge, part):
        return EDGES[edge][1] < FAR or part == side

    def send_on(side, distance, part):
        for edge, (near, far) in enumerate(EDGES):
            if near == distance and taken(side, edge, part):
                along(side, edge, part).start()
                if far == FAR:
                    to_far_pair(side).start()

    sample = lax.broadcasted_iota(jnp.int32, (SAMPLES, WIDTH), 0)

    def patch(half, index):
        live = counts_ref[index]
        sides = []
        for k in range(SLOTS):
            block = jnp.where(k < live, lists_ref[k, index], PLANE)
            sides.append(halves[half][block])
        columns = jnp.concatenate(sides, axis=0)
        strain = jnp.concatenate([shapes[index, k] for k in range(SLOTS)], axis=1)
        both = jnp.dot(strain, columns, preferred_element_type=F32)
        cross = 0.0
        for at in (0, WIDTH):
            part = both[:, at : at + WIDTH]
            cross = cross + part * pltpu.roll(part, WIDTH - 8, 1)
        cross = jnp.where(sample < sizes_ref[index], cross, 0.0)
        part = jnp.sum(cross.reshape(SAMPLES // 8, 8, WIDTH), axis=0)
        if half == 0:
            acc[index] = part
        else:
            folded[index] = jnp.sum(acc[index] + part, axis=0, keepdims=True)

    def work(half, share, shares):
        length = 2 * UNROLL if shares == 1 else UNROLL
        turns = PATCHES // length // shares

        def turn(step, carry):
            for u in range(length):
                patch(half, step * length + u)
            return carry

        lax.fori_loop(share * turns, (share + 1) * turns, turn, 0)

    def pair_wait(slot):
        if slot == 2 * FAR - 1:
            for side in range(2):
                to_far_pair(side).wait_recv()
        else:
            to_pair(slot).wait_recv()

    def turn_over(quarter):
        for slot in range(quarter * QUARTERS, (quarter + 1) * QUARTERS):
            pair_wait(slot)
        x = quarters[quarter]
        turned = halves[quarter // 2]
        at = quarter % 2 * WIDTH

        def block(b, carry):
            turned[b, :, at : at + WIDTH] = x[b].reshape(WIDTH, WIDTH).T
            return carry

        lax.fori_loop(0, PLANE, block, 0, unroll=4)

    for at, dz in enumerate(planes):
        mix_wait(at, dz, mix_recv)
        if abs(dz) == REACH:
            for part in range(2):
                send_on(0 if dz > 0 else 1, REACH, part)
        to_pair(arrives(dz) if dz else 0).start()
    for copy in inputs[3:]:
        copy.wait()

    tasks = {
        1: [lambda: turn_over(0)],
        2: [lambda: turn_over(1), lambda: work(0, 0, 6)],
        3: [lambda: work(0, 1, 6), lambda: work(0, 2, 6)],
        4: [lambda: work(0, 3, 6), lambda: turn_over(2), lambda: work(0, 4, 6), lambda: work(0, 5, 6)],
    }
    for edge, (_, far) in enumerate(EDGES):
        pending = list(tasks.get(edge, ()))
        for part in range(2):
            for side in range(2):
                if taken(side, edge, part):
                    along(side, edge, part).wait_recv()
                    if far < FAR:
                        send_on(side, far, part)
                        if part == 1:
                            to_pair(slot_of(far, side)).start()
            if part == 0 and len(pending) > 1 and edge > 2:
                pending.pop(0)()
        for task in pending:
            task()
    turn_over(3)
    work(1, 0, 1)

    lanes = lax.broadcasted_iota(jnp.int32, (PATCHES, WIDTH), 1)
    terms = jnp.where(lanes // 8 % 2 == 0, folded[...].reshape(PATCHES, WIDTH), 0.0)
    terms = jnp.sum(terms, axis=1, keepdims=True) * scale
    spread = terms * to_lane
    high = spread.astype(BF16)
    rest = spread - high.astype(F32)
    middle = rest.astype(BF16)
    low = (rest - middle.astype(F32)).astype(BF16)
    placed = sum(
        lax.dot_general(to_device, piece, (((1,), (0,)), ((), ())), preferred_element_type=F32)
        for piece in (low, middle, high)
    )
    dense[...] = placed.reshape(COLUMN, 1, WIDTH)

    def column(i):
        d = COLUMN // 2 + (1 - 2 * lax.rem(i, 2)) * lax.div(i, 2)
        there = lax.rem(p + d, COLUMN)
        return pltpu.make_async_remote_copy(
            src_ref=dense.at[there],
            dst_ref=got_column.at[d - 1],
            send_sem=column_send.at[d - 1],
            recv_sem=column_recv,
            device_id=(q, there),
            device_id_type=MESH,
        )

    def column_start(d, carry):
        column(d).start()
        return carry

    lax.fori_loop(1, COLUMN, column_start, 0)
    pltpu.make_async_copy(got_column, got_column, column_recv).wait()
    row[...] = dense[p] + jnp.sum(got_column[...], axis=0)

    def plane(d):
        return pltpu.make_async_remote_copy(
            src_ref=row,
            dst_ref=got_plane.at[d - 1],
            send_sem=plane_send.at[d - 1],
            recv_sem=plane_recv,
            device_id=(lax.rem(q + d, PLANE), p),
            device_id_type=MESH,
        )

    def plane_start(d, carry):
        plane(d).start()
        return carry

    lax.fori_loop(1, PLANE, plane_start, 0)
    pltpu.make_async_copy(got_plane, got_plane, plane_recv).wait()
    total = row[...] + jnp.sum(got_plane[...], axis=0)
    out_ref[...] = total[:, :PATCHES]

    def column_sent(d, carry):
        column(d).wait_send()
        return carry

    def plane_sent(d, carry):
        plane(d).wait_send()
        return carry

    for at, dz in enumerate(planes):
        mix_wait(at, dz, mix_send)
    for edge in range(len(EDGES)):
        for part in range(2):
            for side in range(2):
                if taken(side, edge, part):
                    along(side, edge, part).wait_send()
    for side in range(2):
        to_far_pair(side).wait_send()
    for slot in range(2 * FAR - 1):
        to_pair(slot).wait_send()
    lax.fori_loop(1, COLUMN, column_sent, 0)
    lax.fori_loop(1, PLANE, plane_sent, 0)


def body(responses, adjoints, patch_shapes, block_lists, block_counts, patch_sizes, owner_map):
    freqs = responses.shape[0] * COLUMN
    scale = (SAMPLES * freqs) ** (-0.5)
    vmem = pl.BlockSpec(memory_space=pltpu.VMEM)
    quarter = pltpu.VMEM((PLANE, 2, QUARTERS, PIECE, WIDTH), BF16)
    dma = pltpu.SemaphoreType.DMA
    rows = responses.shape[0] * 2
    out = pl.pallas_call(
        functools.partial(kernel, scale),
        out_shape=jax.ShapeDtypeStruct((1, PATCHES), F32),
        in_specs=[pl.BlockSpec(memory_space=pltpu.HBM)] * 7,
        out_specs=vmem,
        scratch_shapes=[
            pltpu.VMEM((rows, WIDTH), BF16),
            pltpu.VMEM((rows, WIDTH), BF16),
            pltpu.SMEM((SLOTS, PATCHES), jnp.int32),
            pltpu.SMEM((PATCHES,), jnp.int32),
            pltpu.SMEM((PATCHES,), jnp.int32),
            pltpu.VMEM((1, PATCHES), jnp.int32),
            dma((7,)),
            pltpu.VMEM((PLANE, PIECE, WIDTH), BF16),
            quarter,
            quarter,
            quarter,
            quarter,
            pltpu.VMEM((PLANE + 1, WIDTH, 2 * WIDTH), BF16),
            pltpu.VMEM((PLANE + 1, WIDTH, 2 * WIDTH), BF16),
            pltpu.VMEM(patch_shapes.shape, BF16),
            pltpu.VMEM((PATCHES, 8, WIDTH), F32),
            pltpu.VMEM((PATCHES, 1, WIDTH), F32),
            pltpu.VMEM((COLUMN, 1, WIDTH), F32),
            pltpu.VMEM((COLUMN - 1, 1, WIDTH), F32),
            pltpu.VMEM((1, WIDTH), F32),
            pltpu.VMEM((PLANE - 1, 1, WIDTH), F32),
            dma((2 * REACH + 1,)),
            dma((2 * REACH + 1,)),
            dma((2, len(EDGES), 2)),
            dma((2, len(EDGES), 2)),
            dma((2,)),
            dma((2,)),
            dma((2 * FAR - 1,)),
            dma((2 * FAR - 1,)),
            dma((COLUMN - 1,)),
            dma,
            dma((PLANE - 1,)),
            dma,
        ],
        compiler_params=pltpu.CompilerParams(
            collective_id=0, has_side_effects=True, vmem_limit_bytes=58 * 1024 * 1024
        ),
        cost_estimate=pl.CostEstimate(flops=2415919104, bytes_accessed=5000000, transcendentals=0),
    )(
        responses.reshape(rows, WIDTH),
        adjoints.reshape(rows, WIDTH),
        block_lists.T,
        block_counts,
        patch_sizes,
        owner_map.reshape(1, -1),
        patch_shapes,
    )
    return out.reshape(-1)


def solution(mesh):
    placed = (
        P("patch", None, "freq"),
        P("patch", None, "freq"),
        P("patch", None, None, None),
        P("patch", None),
        P("patch"),
        P("patch"),
        P("patch"),
    )
    return jax.shard_map(body, mesh=mesh, in_specs=placed, out_specs=P("patch"), check_vma=False)
```

```python
import functools

import jax
import jax.numpy as jnp
from jax import lax
from jax.experimental import pallas as pl
from jax.experimental.pallas import tpu as pltpu
from jax.sharding import PartitionSpec as P

MESH = pl.DeviceIdType.MESH
F32 = jnp.float32
BF16 = jnp.bfloat16

PLANE = 16
COLUMN = 32
RING = 16
PATCHES = 96
SLOTS = 4
SAMPLES = 48
WIDTH = 128
PIECE = 16
QUARTERS = 4
UNROLL = 16


EDGES = ((2, 3), (2, 5), (3, 4), (5, 6), (5, 8), (6, 7))
LAST = 7
REACH = 2
FAR = RING // 2
ARRIVAL = (1, 2, 3, 5, 4, 6, 7)


def slot_of(distance, side):
    if distance == 0:
        return 0
    if distance == FAR:
        return 2 * FAR - 1
    return 1 + 2 * ARRIVAL.index(distance) + side


def kernel(
    scale,
    resp_hbm,
    adjo_hbm,
    lists_hbm,
    counts_hbm,
    sizes_hbm,
    owner_hbm,
    shapes_hbm,
    out_ref,
    resp_ref,
    adjo_ref,
    lists_ref,
    counts_ref,
    sizes_ref,
    owner_ref,
    input_sem,
    staged,
    x0,
    x1,
    x2,
    x3,
    turned0,
    turned1,
    shapes,
    acc,
    folded,
    dense,
    got_column,
    row,
    got_plane,
    mix_send,
    mix_recv,
    ring_send,
    ring_recv,
    far_send,
    far_recv,
    pair_send,
    pair_recv,
    column_send,
    column_recv,
    plane_send,
    plane_recv,
):
    quarters = (x0, x1, x2, x3)
    halves = (turned0, turned1)
    q = lax.axis_index("freq")
    p = lax.axis_index("patch")
    pair = (q, p + 1 - 2 * lax.rem(p, 2))

    planes = tuple(sorted(range(-REACH, REACH + 1), key=lambda dz: -abs(dz)))

    def shifted(dz):
        return lax.rem(p + COLUMN + 2 * dz, COLUMN)

    inputs = [
        pltpu.make_async_copy(source, target, input_sem.at[at])
        for at, (source, target) in enumerate(
            (
                (resp_hbm, resp_ref),
                (adjo_hbm, adjo_ref),
                (owner_hbm, owner_ref),
                (lists_hbm, lists_ref),
                (counts_hbm, counts_ref),
                (sizes_hbm, sizes_ref),
                (shapes_hbm, shapes),
            )
        )
    ]
    for copy in inputs[:2]:
        copy.start()

    barrier = pltpu.get_barrier_semaphore()
    greeted = 0
    for dz in planes:

        def greet(d, carry, dz=dz):
            pl.semaphore_signal(barrier, inc=1, device_id=(lax.rem(q + d, PLANE), shifted(dz)), device_id_type=MESH)
            return carry

        lax.fori_loop(0 if dz else 1, PLANE, greet, 0)
        greeted += PLANE if dz else PLANE - 1
    for there in (pair, (q, shifted(3)), (q, shifted(-3)), (q, lax.rem(pair[1] + 2, COLUMN)), (q, lax.rem(pair[1] + COLUMN - 2, COLUMN))):
        pl.semaphore_signal(barrier, inc=1, device_id=there, device_id_type=MESH)
        greeted += 1
    for copy in inputs[2:]:
        copy.start()
    for copy in inputs[:2]:
        copy.wait()

    resp = resp_ref[...].astype(F32).reshape(PLANE, 8, WIDTH)
    adjo = adjo_ref[...].astype(F32)
    odd = lax.broadcasted_iota(jnp.int32, adjo.shape, 0) % 2 == 1
    rows = adjo.shape[0]
    swapped = jnp.where(odd, -pltpu.roll(adjo, 1, 0), pltpu.roll(adjo, rows - 1, 0)).reshape(PLANE, 8, WIDTH)
    staged[...] = jnp.concatenate([resp, swapped], axis=1).astype(BF16)
    x0[q, 0, 0] = staged[q]

    pl.semaphore_wait(barrier, greeted)

    def chunk(core, slot, part=None):
        x = quarters[slot // QUARTERS]
        blocks = pl.ds(0, PLANE) if part is None else pl.ds(part * (PLANE // 2), PLANE // 2)
        return x.at[blocks, core, slot % QUARTERS]

    def arrives(dz):
        return slot_of(abs(dz), 0 if dz > 0 else 1)

    for at, dz in enumerate(planes):

        def mix_start(d, carry, at=at, dz=dz):
            there = lax.rem(q + d, PLANE)
            slot = arrives(dz)
            pltpu.make_async_remote_copy(
                src_ref=staged.at[there],
                dst_ref=quarters[slot // QUARTERS].at[q, 0, slot % QUARTERS],
                send_sem=mix_send.at[at],
                recv_sem=mix_recv.at[at],
                device_id=(there, shifted(dz)),
                device_id_type=MESH,
            ).start()
            return carry

        lax.fori_loop(0 if dz else 1, PLANE, mix_start, 0)

    def mix_wait(at, dz, sems):
        pieces = staged if dz else staged.at[pl.ds(0, PLANE - 1)]
        pltpu.make_async_copy(pieces, pieces, sems.at[at]).wait()

    for turned in halves:
        turned[PLANE] = jnp.zeros(turned.shape[1:], BF16)
    inputs[2].wait()

    owner_row = owner_ref[...].astype(F32)
    eye = lax.broadcasted_iota(jnp.int32, (PATCHES, PATCHES), 0) == lax.broadcasted_iota(jnp.int32, (PATCHES, PATCHES), 1)
    owner_column = jnp.sum(jnp.where(eye, jnp.broadcast_to(owner_row, (PATCHES, PATCHES)), 0.0), axis=1, keepdims=True)
    first = lax.broadcasted_iota(jnp.int32, (COLUMN, PATCHES), 0).astype(F32) * PATCHES
    owner_rows = jnp.broadcast_to(owner_row, (COLUMN, PATCHES))
    to_device = jnp.where((owner_rows >= first) & (owner_rows < first + PATCHES), 1.0, 0.0).astype(BF16)
    place = owner_column - jnp.floor((owner_column + 0.5) * (1.0 / PATCHES)) * PATCHES
    lane = lax.broadcasted_iota(jnp.int32, (PATCHES, WIDTH), 1).astype(F32)
    to_lane = jnp.where(place == lane, 1.0, 0.0)

    def along(side, edge, part):
        near, far = EDGES[edge]
        step = 2 * (far - near) * (1 - 2 * side)
        return pltpu.make_async_remote_copy(
            src_ref=chunk(0, slot_of(near, side), part),
            dst_ref=chunk(0, slot_of(far, side), part),
            send_sem=ring_send.at[side, edge, part],
            recv_sem=ring_recv.at[side, edge, part],
            device_id=(q, lax.rem(p + COLUMN + step, COLUMN)),
            device_id_type=MESH,
        )

    def to_far_pair(side, part):
        return pltpu.make_async_remote_copy(
            src_ref=chunk(0, slot_of(LAST - 1, side), part),
            dst_ref=chunk(1, slot_of(LAST, side), part),
            send_sem=far_send.at[side, part],
            recv_sem=far_recv.at[side, part],
            device_id=(q, lax.rem(pair[1] + COLUMN + 2 * (1 - 2 * side), COLUMN)),
            device_id_type=MESH,
        )

    def to_pair(slot):
        return pltpu.make_async_remote_copy(
            src_ref=chunk(0, slot),
            dst_ref=chunk(1, slot),
            send_sem=pair_send.at[slot],
            recv_sem=pair_recv.at[slot],
            device_id=pair,
            device_id_type=MESH,
        )

    def taken(side, edge, part):
        return EDGES[edge][1] < FAR or part == side

    def send_on(side, distance, part):
        for edge, (near, far) in enumerate(EDGES):
            if near == distance and taken(side, edge, part):
                along(side, edge, part).start()
                if far == LAST:
                    to_far_pair(side, part).start()

    sample = lax.broadcasted_iota(jnp.int32, (SAMPLES, WIDTH), 0)

    def patch(half, index):
        live = counts_ref[index]
        sides = []
        for k in range(SLOTS):
            block = jnp.where(k < live, lists_ref[k, index], PLANE)
            sides.append(halves[half][block])
        columns = jnp.concatenate(sides, axis=0)
        strain = jnp.concatenate([shapes[index, k] for k in range(SLOTS)], axis=1)
        both = jnp.dot(strain, columns, preferred_element_type=F32)
        cross = 0.0
        for at in (0, WIDTH):
            part = both[:, at : at + WIDTH]
            cross = cross + part * pltpu.roll(part, WIDTH - 8, 1)
        cross = jnp.where(sample < sizes_ref[index], cross, 0.0)
        part = jnp.sum(cross.reshape(SAMPLES // 8, 8, WIDTH), axis=0)
        if half == 0:
            acc[index] = part
        else:
            folded[pl.ds(index, 1)] = jnp.sum(acc[index] + part, axis=0, keepdims=True)

    def work(half, share, shares):
        length = 2 * UNROLL if shares == 1 else UNROLL
        turns = PATCHES // length // shares

        def turn(step, carry):
            for u in range(length):
                patch(half, step * length + u)
            return carry

        lax.fori_loop(share * turns, (share + 1) * turns, turn, 0)

    direct = (slot_of(LAST, 0), slot_of(LAST, 1))

    def pair_wait(slot):
        if slot in direct:
            for part in range(2):
                to_far_pair(direct.index(slot), part).wait_recv()
        else:
            to_pair(slot).wait_recv()

    def turn_over(quarter):
        for slot in range(quarter * QUARTERS, (quarter + 1) * QUARTERS):
            pair_wait(slot)
        x = quarters[quarter]
        turned = halves[quarter // 2]
        at = quarter % 2 * WIDTH

        def block(b, carry):
            turned[b, :, at : at + WIDTH] = x[b].reshape(WIDTH, WIDTH).T
            return carry

        lax.fori_loop(0, PLANE, block, 0, unroll=4)

    for at, dz in enumerate(planes):
        mix_wait(at, dz, mix_recv)
        if abs(dz) == REACH:
            for part in range(2):
                send_on(0 if dz > 0 else 1, REACH, part)
        to_pair(arrives(dz) if dz else 0).start()
    for copy in inputs[3:]:
        copy.wait()

    tasks = {
        1: [lambda: turn_over(0)],
        2: [lambda: turn_over(1), lambda: work(0, 0, 6)],
        3: [lambda: work(0, 1, 6), lambda: work(0, 2, 6), lambda: work(0, 3, 6)],
        4: [lambda: work(0, 4, 6), lambda: work(0, 5, 6), lambda: turn_over(2)],
    }
    for edge, (_, far) in enumerate(EDGES):
        for part in range(2):
            for side in range(2):
                if taken(side, edge, part):
                    along(side, edge, part).wait_recv()
                    send_on(side, far, part)
                    if part == 1 and far not in (LAST, FAR):
                        to_pair(slot_of(far, side)).start()
        if far == FAR:
            to_pair(slot_of(FAR, 0)).start()
        for task in tasks.get(edge, ()):
            task()
    turn_over(3)
    work(1, 0, 1)

    lanes = lax.broadcasted_iota(jnp.int32, (PATCHES, WIDTH), 1)
    terms = jnp.where(lanes // 8 % 2 == 0, folded[...], 0.0)
    terms = jnp.sum(terms, axis=1, keepdims=True) * scale
    spread = terms * to_lane
    high = spread.astype(BF16)
    rest = spread - high.astype(F32)
    middle = rest.astype(BF16)
    low = (rest - middle.astype(F32)).astype(BF16)
    placed = sum(
        lax.dot_general(to_device, piece, (((1,), (0,)), ((), ())), preferred_element_type=F32)
        for piece in (low, middle, high)
    )
    dense[...] = placed.reshape(COLUMN, 1, WIDTH)

    def column(i):
        d = COLUMN // 2 + (1 - 2 * lax.rem(i, 2)) * lax.div(i, 2)
        there = lax.rem(p + d, COLUMN)
        return pltpu.make_async_remote_copy(
            src_ref=dense.at[there],
            dst_ref=got_column.at[d - 1],
            send_sem=column_send.at[d - 1],
            recv_sem=column_recv,
            device_id=(q, there),
            device_id_type=MESH,
        )

    def column_start(d, carry):
        column(d).start()
        return carry

    lax.fori_loop(1, COLUMN, column_start, 0)
    pltpu.make_async_copy(got_column, got_column, column_recv).wait()
    row[...] = dense[p] + jnp.sum(got_column[...], axis=0)

    def plane(d):
        return pltpu.make_async_remote_copy(
            src_ref=row,
            dst_ref=got_plane.at[d - 1],
            send_sem=plane_send.at[d - 1],
            recv_sem=plane_recv,
            device_id=(lax.rem(q + d, PLANE), p),
            device_id_type=MESH,
        )

    def plane_start(d, carry):
        plane(d).start()
        return carry

    lax.fori_loop(1, PLANE, plane_start, 0)
    pltpu.make_async_copy(got_plane, got_plane, plane_recv).wait()
    total = row[...] + jnp.sum(got_plane[...], axis=0)
    out_ref[...] = total[:, :PATCHES]

    def column_sent(d, carry):
        column(d).wait_send()
        return carry

    def plane_sent(d, carry):
        plane(d).wait_send()
        return carry

    for at, dz in enumerate(planes):
        mix_wait(at, dz, mix_send)
    for edge in range(len(EDGES)):
        for part in range(2):
            for side in range(2):
                if taken(side, edge, part):
                    along(side, edge, part).wait_send()
    for slot in range(2 * FAR):
        if slot in direct:
            for part in range(2):
                to_far_pair(direct.index(slot), part).wait_send()
        else:
            to_pair(slot).wait_send()
    lax.fori_loop(1, COLUMN, column_sent, 0)
    lax.fori_loop(1, PLANE, plane_sent, 0)


def body(responses, adjoints, patch_shapes, block_lists, block_counts, patch_sizes, owner_map):
    freqs = responses.shape[0] * COLUMN
    scale = (SAMPLES * freqs) ** (-0.5)
    vmem = pl.BlockSpec(memory_space=pltpu.VMEM)
    quarter = pltpu.VMEM((PLANE, 2, QUARTERS, PIECE, WIDTH), BF16)
    dma = pltpu.SemaphoreType.DMA
    rows = responses.shape[0] * 2
    out = pl.pallas_call(
        functools.partial(kernel, scale),
        out_shape=jax.ShapeDtypeStruct((1, PATCHES), F32),
        in_specs=[pl.BlockSpec(memory_space=pltpu.HBM)] * 7,
        out_specs=vmem,
        scratch_shapes=[
            pltpu.VMEM((rows, WIDTH), BF16),
            pltpu.VMEM((rows, WIDTH), BF16),
            pltpu.SMEM((SLOTS, PATCHES), jnp.int32),
            pltpu.SMEM((PATCHES,), jnp.int32),
            pltpu.SMEM((PATCHES,), jnp.int32),
            pltpu.VMEM((1, PATCHES), jnp.int32),
            dma((7,)),
            pltpu.VMEM((PLANE, PIECE, WIDTH), BF16),
            quarter,
            quarter,
            quarter,
            quarter,
            pltpu.VMEM((PLANE + 1, WIDTH, 2 * WIDTH), BF16),
            pltpu.VMEM((PLANE + 1, WIDTH, 2 * WIDTH), BF16),
            pltpu.VMEM(patch_shapes.shape, BF16),
            pltpu.VMEM((PATCHES, 8, WIDTH), F32),
            pltpu.VMEM((PATCHES, WIDTH), F32),
            pltpu.VMEM((COLUMN, 1, WIDTH), F32),
            pltpu.VMEM((COLUMN - 1, 1, WIDTH), F32),
            pltpu.VMEM((1, WIDTH), F32),
            pltpu.VMEM((PLANE - 1, 1, WIDTH), F32),
            dma((2 * REACH + 1,)),
            dma((2 * REACH + 1,)),
            dma((2, len(EDGES), 2)),
            dma((2, len(EDGES), 2)),
            dma((2, 2)),
            dma((2, 2)),
            dma((2 * FAR,)),
            dma((2 * FAR,)),
            dma((COLUMN - 1,)),
            dma,
            dma((PLANE - 1,)),
            dma,
        ],
        compiler_params=pltpu.CompilerParams(
            collective_id=0, has_side_effects=True, vmem_limit_bytes=58 * 1024 * 1024
        ),
        cost_estimate=pl.CostEstimate(flops=2415919104, bytes_accessed=5000000, transcendentals=0),
    )(
        responses.reshape(rows, WIDTH),
        adjoints.reshape(rows, WIDTH),
        block_lists.T,
        block_counts,
        patch_sizes,
        owner_map.reshape(1, -1),
        patch_shapes,
    )
    return out.reshape(-1)


def solution(mesh):
    placed = (
        P("patch", None, "freq"),
        P("patch", None, "freq"),
        P("patch", None, None, None),
        P("patch", None),
        P("patch"),
        P("patch"),
        P("patch"),
    )
    return jax.shard_map(body, mesh=mesh, in_specs=placed, out_specs=P("patch"), check_vma=False)
```

```python
import functools

import jax
import jax.numpy as jnp
from jax import lax
from jax.experimental import pallas as pl
from jax.experimental.pallas import tpu as pltpu
from jax.sharding import PartitionSpec as P

MESH = pl.DeviceIdType.MESH
F32 = jnp.float32
BF16 = jnp.bfloat16

PLANE = 16
COLUMN = 32
RING = 16
PATCHES = 96
SLOTS = 4
SAMPLES = 48
WIDTH = 128
PIECE = 16
QUARTERS = 4
UNROLL = 16


EDGES = ((2, 3), (2, 5), (3, 4), (5, 6), (5, 8), (6, 7))
LAST = 7
REACH = 2
FAR = RING // 2
ARRIVAL = (1, 2, 3, 5, 4, 6, 7)


def slot_of(distance, side):
    if distance == 0:
        return 0
    if distance == FAR:
        return 2 * FAR - 1
    return 1 + 2 * ARRIVAL.index(distance) + side


def kernel(
    scale,
    resp_hbm,
    adjo_hbm,
    lists_hbm,
    counts_hbm,
    sizes_hbm,
    owner_hbm,
    shapes_hbm,
    out_ref,
    resp_ref,
    adjo_ref,
    lists_ref,
    counts_ref,
    sizes_ref,
    owner_ref,
    input_sem,
    staged,
    x0,
    x1,
    x2,
    x3,
    turned0,
    turned1,
    shapes,
    acc,
    folded,
    dense,
    got_column,
    row,
    got_plane,
    mix_send,
    mix_recv,
    ring_send,
    ring_recv,
    far_send,
    far_recv,
    pair_send,
    pair_recv,
    column_send,
    column_recv,
    plane_send,
    plane_recv,
):
    quarters = (x0, x1, x2, x3)
    halves = (turned0, turned1)
    q = lax.axis_index("freq")
    p = lax.axis_index("patch")
    pair = (q, p + 1 - 2 * lax.rem(p, 2))

    planes = tuple(sorted(range(-REACH, REACH + 1), key=lambda dz: -abs(dz)))

    def shifted(dz):
        return lax.rem(p + COLUMN + 2 * dz, COLUMN)

    inputs = [
        pltpu.make_async_copy(source, target, input_sem.at[at])
        for at, (source, target) in enumerate(
            (
                (resp_hbm, resp_ref),
                (adjo_hbm, adjo_ref),
                (owner_hbm, owner_ref),
                (lists_hbm, lists_ref),
                (counts_hbm, counts_ref),
                (sizes_hbm, sizes_ref),
                (shapes_hbm, shapes),
            )
        )
    ]
    for copy in inputs[:2]:
        copy.start()

    barrier = pltpu.get_barrier_semaphore()
    greeted = 0
    for dz in planes:

        def greet(d, carry, dz=dz):
            pl.semaphore_signal(barrier, inc=1, device_id=(lax.rem(q + d, PLANE), shifted(dz)), device_id_type=MESH)
            return carry

        lax.fori_loop(0 if dz else 1, PLANE, greet, 0)
        greeted += PLANE if dz else PLANE - 1
    for there in (pair, (q, shifted(3)), (q, shifted(-3)), (q, lax.rem(pair[1] + 2, COLUMN)), (q, lax.rem(pair[1] + COLUMN - 2, COLUMN))):
        pl.semaphore_signal(barrier, inc=1, device_id=there, device_id_type=MESH)
        greeted += 1
    for copy in inputs[2:]:
        copy.start()
    for copy in inputs[:2]:
        copy.wait()

    resp = resp_ref[...].astype(F32).reshape(PLANE, 8, WIDTH)
    adjo = adjo_ref[...].astype(F32)
    odd = lax.broadcasted_iota(jnp.int32, adjo.shape, 0) % 2 == 1
    rows = adjo.shape[0]
    swapped = jnp.where(odd, -pltpu.roll(adjo, 1, 0), pltpu.roll(adjo, rows - 1, 0)).reshape(PLANE, 8, WIDTH)
    staged[...] = jnp.concatenate([resp, swapped], axis=1).astype(BF16)
    x0[q, 0, 0] = staged[q]

    pl.semaphore_wait(barrier, greeted)

    def chunk(core, slot, part=None):
        x = quarters[slot // QUARTERS]
        blocks = pl.ds(0, PLANE) if part is None else pl.ds(part * (PLANE // 2), PLANE // 2)
        return x.at[blocks, core, slot % QUARTERS]

    def arrives(dz):
        return slot_of(abs(dz), 0 if dz > 0 else 1)

    for at, dz in enumerate(planes):

        def mix_start(d, carry, at=at, dz=dz):
            there = lax.rem(q + d + PLANE // 2, PLANE) if dz else lax.rem(q + d, PLANE)
            slot = arrives(dz)
            pltpu.make_async_remote_copy(
                src_ref=staged.at[there],
                dst_ref=quarters[slot // QUARTERS].at[q, 0, slot % QUARTERS],
                send_sem=mix_send.at[at],
                recv_sem=mix_recv.at[at],
                device_id=(there, shifted(dz)),
                device_id_type=MESH,
            ).start()
            return carry

        lax.fori_loop(0 if dz else 1, PLANE, mix_start, 0)

    def mix_wait(at, dz, sems):
        pieces = staged if dz else staged.at[pl.ds(0, PLANE - 1)]
        pltpu.make_async_copy(pieces, pieces, sems.at[at]).wait()

    for turned in halves:
        turned[PLANE] = jnp.zeros(turned.shape[1:], BF16)
    inputs[2].wait()

    owner_row = owner_ref[...].astype(F32)
    eye = lax.broadcasted_iota(jnp.int32, (PATCHES, PATCHES), 0) == lax.broadcasted_iota(jnp.int32, (PATCHES, PATCHES), 1)
    owner_column = jnp.sum(jnp.where(eye, jnp.broadcast_to(owner_row, (PATCHES, PATCHES)), 0.0), axis=1, keepdims=True)
    first = lax.broadcasted_iota(jnp.int32, (COLUMN, PATCHES), 0).astype(F32) * PATCHES
    owner_rows = jnp.broadcast_to(owner_row, (COLUMN, PATCHES))
    to_device = jnp.where((owner_rows >= first) & (owner_rows < first + PATCHES), 1.0, 0.0).astype(BF16)
    place = owner_column - jnp.floor((owner_column + 0.5) * (1.0 / PATCHES)) * PATCHES
    lane = lax.broadcasted_iota(jnp.int32, (PATCHES, WIDTH), 1).astype(F32)
    to_lane = jnp.where(place == lane, 1.0, 0.0)

    def along(side, edge, part):
        near, far = EDGES[edge]
        step = 2 * (far - near) * (1 - 2 * side)
        return pltpu.make_async_remote_copy(
            src_ref=chunk(0, slot_of(near, side), part),
            dst_ref=chunk(0, slot_of(far, side), part),
            send_sem=ring_send.at[side, edge, part],
            recv_sem=ring_recv.at[side, edge, part],
            device_id=(q, lax.rem(p + COLUMN + step, COLUMN)),
            device_id_type=MESH,
        )

    def to_far_pair(side, part):
        return pltpu.make_async_remote_copy(
            src_ref=chunk(0, slot_of(LAST - 1, side), part),
            dst_ref=chunk(1, slot_of(LAST, side), part),
            send_sem=far_send.at[side, part],
            recv_sem=far_recv.at[side, part],
            device_id=(q, lax.rem(pair[1] + COLUMN + 2 * (1 - 2 * side), COLUMN)),
            device_id_type=MESH,
        )

    def to_pair(slot):
        return pltpu.make_async_remote_copy(
            src_ref=chunk(0, slot),
            dst_ref=chunk(1, slot),
            send_sem=pair_send.at[slot],
            recv_sem=pair_recv.at[slot],
            device_id=pair,
            device_id_type=MESH,
        )

    def taken(side, edge, part):
        return EDGES[edge][1] < FAR or part == side

    def send_on(side, distance, part):
        for edge, (near, far) in enumerate(EDGES):
            if near == distance and taken(side, edge, part):
                along(side, edge, part).start()
                if far == LAST:
                    to_far_pair(side, part).start()

    sample = lax.broadcasted_iota(jnp.int32, (SAMPLES, WIDTH), 0)

    def patch(half, index):
        live = counts_ref[index]
        sides = []
        for k in range(SLOTS):
            block = jnp.where(k < live, lists_ref[k, index], PLANE)
            sides.append(halves[half][block])
        columns = jnp.concatenate(sides, axis=0)
        strain = jnp.concatenate([shapes[index, k] for k in range(SLOTS)], axis=1)
        both = jnp.dot(strain, columns, preferred_element_type=F32)
        cross = 0.0
        for at in (0, WIDTH):
            part = both[:, at : at + WIDTH]
            cross = cross + part * pltpu.roll(part, WIDTH - 8, 1)
        cross = jnp.where(sample < sizes_ref[index], cross, 0.0)
        part = jnp.sum(cross.reshape(SAMPLES // 8, 8, WIDTH), axis=0)
        if half == 0:
            acc[index] = part
        else:
            folded[pl.ds(index, 1)] = jnp.sum(acc[index] + part, axis=0, keepdims=True)

    def work(half, share, shares):
        length = 2 * UNROLL if shares == 1 else UNROLL
        turns = PATCHES // length // shares

        def turn(step, carry):
            for u in range(length):
                patch(half, step * length + u)
            return carry

        lax.fori_loop(share * turns, (share + 1) * turns, turn, 0)

    direct = (slot_of(LAST, 0), slot_of(LAST, 1))

    def pair_wait(slot):
        if slot in direct:
            for part in range(2):
                to_far_pair(direct.index(slot), part).wait_recv()
        else:
            to_pair(slot).wait_recv()

    def turn_over(quarter):
        for slot in range(quarter * QUARTERS, (quarter + 1) * QUARTERS):
            pair_wait(slot)
        x = quarters[quarter]
        turned = halves[quarter // 2]
        at = quarter % 2 * WIDTH

        def block(b, carry):
            turned[b, :, at : at + WIDTH] = x[b].reshape(WIDTH, WIDTH).T
            return carry

        lax.fori_loop(0, PLANE, block, 0, unroll=4)

    for at, dz in enumerate(planes):
        mix_wait(at, dz, mix_recv)
        if abs(dz) == REACH:
            for part in range(2):
                send_on(0 if dz > 0 else 1, REACH, part)
        to_pair(arrives(dz) if dz else 0).start()
    for copy in inputs[3:]:
        copy.wait()

    tasks = {
        0: [lambda: turn_over(0)],
        2: [lambda: turn_over(1), lambda: work(0, 0, 6)],
        3: [lambda: work(0, 1, 6), lambda: work(0, 2, 6), lambda: work(0, 3, 6)],
        4: [lambda: work(0, 4, 6), lambda: work(0, 5, 6), lambda: turn_over(2)],
    }
    for edge, (_, far) in enumerate(EDGES):
        for part in range(2):
            for side in range(2):
                if taken(side, edge, part):
                    along(side, edge, part).wait_recv()
                    send_on(side, far, part)
                    if part == 1 and far not in (LAST, FAR):
                        to_pair(slot_of(far, side)).start()
        if far == FAR:
            to_pair(slot_of(FAR, 0)).start()
        for task in tasks.get(edge, ()):
            task()
    turn_over(3)
    work(1, 0, 1)

    lanes = lax.broadcasted_iota(jnp.int32, (PATCHES, WIDTH), 1)
    terms = jnp.where(lanes // 8 % 2 == 0, folded[...], 0.0)
    terms = jnp.sum(terms, axis=1, keepdims=True) * scale
    spread = terms * to_lane
    high = spread.astype(BF16)
    rest = spread - high.astype(F32)
    middle = rest.astype(BF16)
    low = (rest - middle.astype(F32)).astype(BF16)
    placed = sum(
        lax.dot_general(to_device, piece, (((1,), (0,)), ((), ())), preferred_element_type=F32)
        for piece in (low, middle, high)
    )
    dense[...] = placed.reshape(COLUMN, 1, WIDTH)

    def column(i):
        d = COLUMN // 2 + (1 - 2 * lax.rem(i, 2)) * lax.div(i, 2)
        there = lax.rem(p + d, COLUMN)
        return pltpu.make_async_remote_copy(
            src_ref=dense.at[there],
            dst_ref=got_column.at[d - 1],
            send_sem=column_send.at[d - 1],
            recv_sem=column_recv,
            device_id=(q, there),
            device_id_type=MESH,
        )

    def column_start(d, carry):
        column(d).start()
        return carry

    lax.fori_loop(1, COLUMN, column_start, 0)
    pltpu.make_async_copy(got_column, got_column, column_recv).wait()
    row[...] = dense[p] + jnp.sum(got_column[...], axis=0)

    def plane(d):
        return pltpu.make_async_remote_copy(
            src_ref=row,
            dst_ref=got_plane.at[d - 1],
            send_sem=plane_send.at[d - 1],
            recv_sem=plane_recv,
            device_id=(lax.rem(q + d, PLANE), p),
            device_id_type=MESH,
        )

    def plane_start(d, carry):
        plane(d).start()
        return carry

    lax.fori_loop(1, PLANE, plane_start, 0)
    pltpu.make_async_copy(got_plane, got_plane, plane_recv).wait()
    total = row[...] + jnp.sum(got_plane[...], axis=0)
    out_ref[...] = total[:, :PATCHES]

    def column_sent(d, carry):
        column(d).wait_send()
        return carry

    def plane_sent(d, carry):
        plane(d).wait_send()
        return carry

    for at, dz in enumerate(planes):
        mix_wait(at, dz, mix_send)
    for edge in range(len(EDGES)):
        for part in range(2):
            for side in range(2):
                if taken(side, edge, part):
                    along(side, edge, part).wait_send()
    for slot in range(2 * FAR):
        if slot in direct:
            for part in range(2):
                to_far_pair(direct.index(slot), part).wait_send()
        else:
            to_pair(slot).wait_send()
    lax.fori_loop(1, COLUMN, column_sent, 0)
    lax.fori_loop(1, PLANE, plane_sent, 0)


def body(responses, adjoints, patch_shapes, block_lists, block_counts, patch_sizes, owner_map):
    freqs = responses.shape[0] * COLUMN
    scale = (SAMPLES * freqs) ** (-0.5)
    vmem = pl.BlockSpec(memory_space=pltpu.VMEM)
    quarter = pltpu.VMEM((PLANE, 2, QUARTERS, PIECE, WIDTH), BF16)
    dma = pltpu.SemaphoreType.DMA
    rows = responses.shape[0] * 2
    out = pl.pallas_call(
        functools.partial(kernel, scale),
        out_shape=jax.ShapeDtypeStruct((1, PATCHES), F32),
        in_specs=[pl.BlockSpec(memory_space=pltpu.HBM)] * 7,
        out_specs=vmem,
        scratch_shapes=[
            pltpu.VMEM((rows, WIDTH), BF16),
            pltpu.VMEM((rows, WIDTH), BF16),
            pltpu.SMEM((SLOTS, PATCHES), jnp.int32),
            pltpu.SMEM((PATCHES,), jnp.int32),
            pltpu.SMEM((PATCHES,), jnp.int32),
            pltpu.VMEM((1, PATCHES), jnp.int32),
            dma((7,)),
            pltpu.VMEM((PLANE, PIECE, WIDTH), BF16),
            quarter,
            quarter,
            quarter,
            quarter,
            pltpu.VMEM((PLANE + 1, WIDTH, 2 * WIDTH), BF16),
            pltpu.VMEM((PLANE + 1, WIDTH, 2 * WIDTH), BF16),
            pltpu.VMEM(patch_shapes.shape, BF16),
            pltpu.VMEM((PATCHES, 8, WIDTH), F32),
            pltpu.VMEM((PATCHES, WIDTH), F32),
            pltpu.VMEM((COLUMN, 1, WIDTH), F32),
            pltpu.VMEM((COLUMN - 1, 1, WIDTH), F32),
            pltpu.VMEM((1, WIDTH), F32),
            pltpu.VMEM((PLANE - 1, 1, WIDTH), F32),
            dma((2 * REACH + 1,)),
            dma((2 * REACH + 1,)),
            dma((2, len(EDGES), 2)),
            dma((2, len(EDGES), 2)),
            dma((2, 2)),
            dma((2, 2)),
            dma((2 * FAR,)),
            dma((2 * FAR,)),
            dma((COLUMN - 1,)),
            dma,
            dma((PLANE - 1,)),
            dma,
        ],
        compiler_params=pltpu.CompilerParams(
            collective_id=0, has_side_effects=True, vmem_limit_bytes=58 * 1024 * 1024
        ),
        cost_estimate=pl.CostEstimate(flops=2415919104, bytes_accessed=5000000, transcendentals=0),
    )(
        responses.reshape(rows, WIDTH),
        adjoints.reshape(rows, WIDTH),
        block_lists.T,
        block_counts,
        patch_sizes,
        owner_map.reshape(1, -1),
        patch_shapes,
    )
    return out.reshape(-1)


def solution(mesh):
    placed = (
        P("patch", None, "freq"),
        P("patch", None, "freq"),
        P("patch", None, None, None),
        P("patch", None),
        P("patch"),
        P("patch"),
        P("patch"),
    )
    return jax.shard_map(body, mesh=mesh, in_specs=placed, out_specs=P("patch"), check_vma=False)
```

```python
import functools

import jax
import jax.numpy as jnp
from jax import lax
from jax.experimental import pallas as pl
from jax.experimental.pallas import tpu as pltpu
from jax.sharding import PartitionSpec as P

MESH = pl.DeviceIdType.MESH
F32 = jnp.float32
BF16 = jnp.bfloat16

PLANE = 16
COLUMN = 32
RING = 16
PATCHES = 96
SLOTS = 4
SAMPLES = 48
WIDTH = 128
PIECE = 16
QUARTERS = 4
UNROLL = 16


EDGES = ((2, 3), (2, 5), (3, 4), (5, 6), (5, 8), (6, 7))
LAST = 7
REACH = 2
FAR = RING // 2
ARRIVAL = (1, 2, 3, 5, 4, 6, 7)


def slot_of(distance, side):
    if distance == 0:
        return 0
    if distance == FAR:
        return 2 * FAR - 1
    return 1 + 2 * ARRIVAL.index(distance) + side


def kernel(
    scale,
    resp_hbm,
    adjo_hbm,
    lists_hbm,
    counts_hbm,
    sizes_hbm,
    owner_hbm,
    shapes_hbm,
    out_ref,
    resp_ref,
    adjo_ref,
    lists_ref,
    counts_ref,
    sizes_ref,
    owner_ref,
    input_sem,
    staged,
    x0,
    x1,
    x2,
    x3,
    turned0,
    turned1,
    shapes,
    acc,
    folded,
    dense,
    got_column,
    row,
    got_plane,
    mix_send,
    mix_recv,
    ring_send,
    ring_recv,
    far_send,
    far_recv,
    pair_send,
    pair_recv,
    column_send,
    column_recv,
    plane_send,
    plane_recv,
):
    quarters = (x0, x1, x2, x3)
    halves = (turned0, turned1)
    q = lax.axis_index("freq")
    p = lax.axis_index("patch")
    pair = (q, p + 1 - 2 * lax.rem(p, 2))

    planes = tuple(sorted(range(-REACH, REACH + 1), key=lambda dz: -abs(dz)))

    def shifted(dz):
        return lax.rem(p + COLUMN + 2 * dz, COLUMN)

    inputs = [
        pltpu.make_async_copy(source, target, input_sem.at[at])
        for at, (source, target) in enumerate(
            (
                (resp_hbm, resp_ref),
                (adjo_hbm, adjo_ref),
                (owner_hbm, owner_ref),
                (lists_hbm, lists_ref),
                (counts_hbm, counts_ref),
                (sizes_hbm, sizes_ref),
                (shapes_hbm, shapes),
            )
        )
    ]
    for copy in inputs[:2]:
        copy.start()

    barrier = pltpu.get_barrier_semaphore()
    greeted = 0
    for dz in planes:

        def greet(d, carry, dz=dz):
            pl.semaphore_signal(barrier, inc=1, device_id=(lax.rem(q + d, PLANE), shifted(dz)), device_id_type=MESH)
            return carry

        lax.fori_loop(0 if dz else 1, PLANE, greet, 0)
        greeted += PLANE if dz else PLANE - 1
    for there in (pair, (q, shifted(3)), (q, shifted(-3)), (q, lax.rem(pair[1] + 2, COLUMN)), (q, lax.rem(pair[1] + COLUMN - 2, COLUMN))):
        pl.semaphore_signal(barrier, inc=1, device_id=there, device_id_type=MESH)
        greeted += 1
    for copy in inputs[2:]:
        copy.start()
    for copy in inputs[:2]:
        copy.wait()

    resp = resp_ref[...].astype(F32).reshape(PLANE, 8, WIDTH)
    adjo = adjo_ref[...].astype(F32)
    odd = lax.broadcasted_iota(jnp.int32, adjo.shape, 0) % 2 == 1
    rows = adjo.shape[0]
    swapped = jnp.where(odd, -pltpu.roll(adjo, 1, 0), pltpu.roll(adjo, rows - 1, 0)).reshape(PLANE, 8, WIDTH)
    staged[...] = jnp.concatenate([resp, swapped], axis=1).astype(BF16)
    x0[q, 0, 0] = staged[q]

    pl.semaphore_wait(barrier, greeted)

    def chunk(core, slot, part=None):
        x = quarters[slot // QUARTERS]
        blocks = pl.ds(0, PLANE) if part is None else pl.ds(part * (PLANE // 2), PLANE // 2)
        return x.at[blocks, core, slot % QUARTERS]

    def arrives(dz):
        return slot_of(abs(dz), 0 if dz > 0 else 1)

    for at, dz in enumerate(planes):

        def mix_start(d, carry, at=at, dz=dz):
            there = lax.rem(q + d + PLANE // 2, PLANE) if dz else lax.rem(q + d, PLANE)
            slot = arrives(dz)
            pltpu.make_async_remote_copy(
                src_ref=staged.at[there],
                dst_ref=quarters[slot // QUARTERS].at[q, 0, slot % QUARTERS],
                send_sem=mix_send.at[at],
                recv_sem=mix_recv.at[at],
                device_id=(there, shifted(dz)),
                device_id_type=MESH,
            ).start()
            return carry

        lax.fori_loop(0 if dz else 1, PLANE, mix_start, 0)

    def mix_wait(at, dz, sems):
        pieces = staged if dz else staged.at[pl.ds(0, PLANE - 1)]
        pltpu.make_async_copy(pieces, pieces, sems.at[at]).wait()

    for turned in halves:
        turned[PLANE] = jnp.zeros(turned.shape[1:], BF16)
    inputs[2].wait()

    owner_row = owner_ref[...].astype(F32)
    eye = lax.broadcasted_iota(jnp.int32, (PATCHES, PATCHES), 0) == lax.broadcasted_iota(jnp.int32, (PATCHES, PATCHES), 1)
    owner_column = jnp.sum(jnp.where(eye, jnp.broadcast_to(owner_row, (PATCHES, PATCHES)), 0.0), axis=1, keepdims=True)
    first = lax.broadcasted_iota(jnp.int32, (COLUMN, PATCHES), 0).astype(F32) * PATCHES
    owner_rows = jnp.broadcast_to(owner_row, (COLUMN, PATCHES))
    to_device = jnp.where((owner_rows >= first) & (owner_rows < first + PATCHES), 1.0, 0.0).astype(BF16)
    place = owner_column - jnp.floor((owner_column + 0.5) * (1.0 / PATCHES)) * PATCHES
    lane = lax.broadcasted_iota(jnp.int32, (PATCHES, WIDTH), 1).astype(F32)
    to_lane = jnp.where(place == lane, 1.0, 0.0)

    def along(side, edge, part):
        near, far = EDGES[edge]
        step = 2 * (far - near) * (1 - 2 * side)
        return pltpu.make_async_remote_copy(
            src_ref=chunk(0, slot_of(near, side), part),
            dst_ref=chunk(0, slot_of(far, side), part),
            send_sem=ring_send.at[side, edge, part],
            recv_sem=ring_recv.at[side, edge, part],
            device_id=(q, lax.rem(p + COLUMN + step, COLUMN)),
            device_id_type=MESH,
        )

    def to_far_pair(side, part):
        return pltpu.make_async_remote_copy(
            src_ref=chunk(0, slot_of(LAST - 1, side), part),
            dst_ref=chunk(1, slot_of(LAST, side), part),
            send_sem=far_send.at[side, part],
            recv_sem=far_recv.at[side, part],
            device_id=(q, lax.rem(pair[1] + COLUMN + 2 * (1 - 2 * side), COLUMN)),
            device_id_type=MESH,
        )

    def to_pair(slot):
        return pltpu.make_async_remote_copy(
            src_ref=chunk(0, slot),
            dst_ref=chunk(1, slot),
            send_sem=pair_send.at[slot],
            recv_sem=pair_recv.at[slot],
            device_id=pair,
            device_id_type=MESH,
        )

    def taken(side, edge, part):
        return EDGES[edge][1] < FAR or part == side

    def send_on(side, distance, part):
        for edge, (near, far) in enumerate(EDGES):
            if near == distance and taken(side, edge, part):
                along(side, edge, part).start()
                if far == LAST:
                    to_far_pair(side, part).start()

    sample = lax.broadcasted_iota(jnp.int32, (SAMPLES, WIDTH), 0)

    def patch(half, index):
        live = counts_ref[index]
        sides = []
        for k in range(SLOTS):
            block = jnp.where(k < live, lists_ref[k, index], PLANE)
            sides.append(halves[half][block])
        columns = jnp.concatenate(sides, axis=0)
        strain = jnp.concatenate([shapes[index, k] for k in range(SLOTS)], axis=1)
        both = jnp.dot(strain, columns, preferred_element_type=F32)
        cross = 0.0
        for at in (0, WIDTH):
            part = both[:, at : at + WIDTH]
            cross = cross + part * pltpu.roll(part, WIDTH - 8, 1)
        cross = jnp.where(sample < sizes_ref[index], cross, 0.0)
        part = jnp.sum(cross.reshape(SAMPLES // 8, 8, WIDTH), axis=0)
        if half == 0:
            acc[index] = part
        else:
            folded[pl.ds(index, 1)] = jnp.sum(acc[index] + part, axis=0, keepdims=True)

    def work(half, share, shares):
        length = 3 * UNROLL if shares == 1 else UNROLL
        turns = PATCHES // length // shares

        def turn(step, carry):
            for u in range(length):
                patch(half, step * length + u)
            return carry

        lax.fori_loop(share * turns, (share + 1) * turns, turn, 0)

    direct = (slot_of(LAST, 0), slot_of(LAST, 1))

    def pair_wait(slot):
        if slot in direct:
            for part in range(2):
                to_far_pair(direct.index(slot), part).wait_recv()
        else:
            to_pair(slot).wait_recv()

    def turn_over(quarter):
        for slot in range(quarter * QUARTERS, (quarter + 1) * QUARTERS):
            pair_wait(slot)
        x = quarters[quarter]
        turned = halves[quarter // 2]
        at = quarter % 2 * WIDTH

        def block(b, carry):
            turned[b, :, at : at + WIDTH] = x[b].reshape(WIDTH, WIDTH).T
            return carry

        lax.fori_loop(0, PLANE, block, 0, unroll=4)

    for at, dz in enumerate(planes):
        mix_wait(at, dz, mix_recv)
        if abs(dz) == REACH:
            for part in range(2):
                send_on(0 if dz > 0 else 1, REACH, part)
        to_pair(arrives(dz) if dz else 0).start()
    for copy in inputs[3:]:
        copy.wait()

    tasks = {
        0: [lambda: turn_over(0)],
        2: [lambda: turn_over(1), lambda: work(0, 0, 6)],
        3: [lambda: work(0, 1, 6), lambda: work(0, 2, 6), lambda: work(0, 3, 6)],
        4: [lambda: work(0, 4, 6), lambda: work(0, 5, 6), lambda: turn_over(2)],
    }
    for edge, (_, far) in enumerate(EDGES):
        for part in range(2):
            for side in range(2):
                if taken(side, edge, part):
                    along(side, edge, part).wait_recv()
                    send_on(side, far, part)
                    if part == 1 and far not in (LAST, FAR):
                        to_pair(slot_of(far, side)).start()
        if far == FAR:
            to_pair(slot_of(FAR, 0)).start()
        for task in tasks.get(edge, ()):
            task()
    turn_over(3)
    work(1, 0, 1)

    lanes = lax.broadcasted_iota(jnp.int32, (PATCHES, WIDTH), 1)
    terms = jnp.where(lanes // 8 % 2 == 0, folded[...], 0.0)
    terms = jnp.sum(terms, axis=1, keepdims=True) * scale
    spread = terms * to_lane
    high = spread.astype(BF16)
    rest = spread - high.astype(F32)
    middle = rest.astype(BF16)
    low = (rest - middle.astype(F32)).astype(BF16)
    placed = sum(
        lax.dot_general(to_device, piece, (((1,), (0,)), ((), ())), preferred_element_type=F32)
        for piece in (low, middle, high)
    )
    dense[...] = placed.reshape(COLUMN, 1, WIDTH)

    def column(i):
        d = COLUMN // 2 + (1 - 2 * lax.rem(i, 2)) * lax.div(i, 2)
        there = lax.rem(p + d, COLUMN)
        return pltpu.make_async_remote_copy(
            src_ref=dense.at[there],
            dst_ref=got_column.at[d - 1],
            send_sem=column_send.at[d - 1],
            recv_sem=column_recv,
            device_id=(q, there),
            device_id_type=MESH,
        )

    def column_start(d, carry):
        column(d).start()
        return carry

    lax.fori_loop(1, COLUMN, column_start, 0)
    pltpu.make_async_copy(got_column, got_column, column_recv).wait()
    row[...] = dense[p] + jnp.sum(got_column[...], axis=0)

    def plane(d):
        return pltpu.make_async_remote_copy(
            src_ref=row,
            dst_ref=got_plane.at[d - 1],
            send_sem=plane_send.at[d - 1],
            recv_sem=plane_recv,
            device_id=(lax.rem(q + d, PLANE), p),
            device_id_type=MESH,
        )

    def plane_start(d, carry):
        plane(d).start()
        return carry

    lax.fori_loop(1, PLANE, plane_start, 0)
    pltpu.make_async_copy(got_plane, got_plane, plane_recv).wait()
    total = row[...] + jnp.sum(got_plane[...], axis=0)
    out_ref[...] = total[:, :PATCHES]

    def column_sent(d, carry):
        column(d).wait_send()
        return carry

    def plane_sent(d, carry):
        plane(d).wait_send()
        return carry

    for at, dz in enumerate(planes):
        mix_wait(at, dz, mix_send)
    for edge in range(len(EDGES)):
        for part in range(2):
            for side in range(2):
                if taken(side, edge, part):
                    along(side, edge, part).wait_send()
    for slot in range(2 * FAR):
        if slot in direct:
            for part in range(2):
                to_far_pair(direct.index(slot), part).wait_send()
        else:
            to_pair(slot).wait_send()
    lax.fori_loop(1, COLUMN, column_sent, 0)
    lax.fori_loop(1, PLANE, plane_sent, 0)


def body(responses, adjoints, patch_shapes, block_lists, block_counts, patch_sizes, owner_map):
    freqs = responses.shape[0] * COLUMN
    scale = (SAMPLES * freqs) ** (-0.5)
    vmem = pl.BlockSpec(memory_space=pltpu.VMEM)
    quarter = pltpu.VMEM((PLANE, 2, QUARTERS, PIECE, WIDTH), BF16)
    dma = pltpu.SemaphoreType.DMA
    rows = responses.shape[0] * 2
    out = pl.pallas_call(
        functools.partial(kernel, scale),
        out_shape=jax.ShapeDtypeStruct((1, PATCHES), F32),
        in_specs=[pl.BlockSpec(memory_space=pltpu.HBM)] * 7,
        out_specs=vmem,
        scratch_shapes=[
            pltpu.VMEM((rows, WIDTH), BF16),
            pltpu.VMEM((rows, WIDTH), BF16),
            pltpu.SMEM((SLOTS, PATCHES), jnp.int32),
            pltpu.SMEM((PATCHES,), jnp.int32),
            pltpu.SMEM((PATCHES,), jnp.int32),
            pltpu.VMEM((1, PATCHES), jnp.int32),
            dma((7,)),
            pltpu.VMEM((PLANE, PIECE, WIDTH), BF16),
            quarter,
            quarter,
            quarter,
            quarter,
            pltpu.VMEM((PLANE + 1, WIDTH, 2 * WIDTH), BF16),
            pltpu.VMEM((PLANE + 1, WIDTH, 2 * WIDTH), BF16),
            pltpu.VMEM(patch_shapes.shape, BF16),
            pltpu.VMEM((PATCHES, 8, WIDTH), F32),
            pltpu.VMEM((PATCHES, WIDTH), F32),
            pltpu.VMEM((COLUMN, 1, WIDTH), F32),
            pltpu.VMEM((COLUMN - 1, 1, WIDTH), F32),
            pltpu.VMEM((1, WIDTH), F32),
            pltpu.VMEM((PLANE - 1, 1, WIDTH), F32),
            dma((2 * REACH + 1,)),
            dma((2 * REACH + 1,)),
            dma((2, len(EDGES), 2)),
            dma((2, len(EDGES), 2)),
            dma((2, 2)),
            dma((2, 2)),
            dma((2 * FAR,)),
            dma((2 * FAR,)),
            dma((COLUMN - 1,)),
            dma,
            dma((PLANE - 1,)),
            dma,
        ],
        compiler_params=pltpu.CompilerParams(
            collective_id=0, has_side_effects=True, vmem_limit_bytes=58 * 1024 * 1024
        ),
        cost_estimate=pl.CostEstimate(flops=2415919104, bytes_accessed=5000000, transcendentals=0),
    )(
        responses.reshape(rows, WIDTH),
        adjoints.reshape(rows, WIDTH),
        block_lists.T,
        block_counts,
        patch_sizes,
        owner_map.reshape(1, -1),
        patch_shapes,
    )
    return out.reshape(-1)


def solution(mesh):
    placed = (
        P("patch", None, "freq"),
        P("patch", None, "freq"),
        P("patch", None, None, None),
        P("patch", None),
        P("patch"),
        P("patch"),
        P("patch"),
    )
    return jax.shard_map(body, mesh=mesh, in_specs=placed, out_specs=P("patch"), check_vma=False)
```
